256 devices in a mesh: space: 32 (over x, z_hi, y), chan: 8 (over z_lo, core).
Axes of the slice: x: 4, y: 4, z: 8 (z_hi: 2, z_lo: 4; z = z_hi * 4 + z_lo), core: 2. Of those that a mesh axis runs over, the one named last changes fastest.
Arguments:
- volume: bfloat16 [64, 64, 32, 128], P('chan', 'space'), may hold values from -6 to 6
- weight_one: bfloat16 [64, 64, 3, 3, 3], P('chan'), may hold values from -0.15625 to 0.15625
- bias_one: float32 [64], P('chan'), may hold values from -0.5 to 0.5
- weight_two: bfloat16 [64, 64, 3, 3, 3], P('chan'), may hold values from -0.15625 to 0.15625
- bias_two: float32 [64], P('chan'), may hold values from -0.5 to 0.5
- cotangent: bfloat16 [64, 64, 32, 128], P('chan', 'space'), may hold values from -6 to 6
Outputs:
- features: bfloat16 [64, 64, 32, 128], P('chan', 'space')
- grad_w_one: float32 [64, 64, 3, 3, 3], P('chan')
- grad_b_one: float32 [64], P('chan')
- grad_w_two: float32 [64, 64, 3, 3, 3], P('chan')
- grad_b_two: float32 [64], P('chan')
The draws below stay inside these ranges and needn't reach their ends.
All inputs are finite; a program needn't handle non-finite values.
Results may differ from the reference program's by a relative error of at most 0.03.
The reference program's roundings to bfloat16 on the way (of `act_one`, `delta_two` and `delta_one`) count: a program that leaves them out, or rounds other values in their place, can miss the bound.
Values may be sent and summed in bfloat16 or wider, within the bound.
No kernel may reach another device: no remote copies, remote signals or barrier semaphores. Data moves between devices by JAX's collectives and lax.ppermute only.
A program may use at most 128 MiB of HBM per device.

```python
import jax
import jax.numpy as jnp
from jax import lax

C = 64
NY = 32
NZ = 128
NX = 64


def levels(stream_key, dims, split, least, largest):
    gain = 1.0
    for position, shards_of in split:
        steps = jax.random.uniform(jax.random.fold_in(jax.random.fold_in(stream_key, 6), position), (shards_of,), jnp.float32, least / len(split), largest / len(split))
        gain = gain * jnp.repeat(jnp.exp(steps), dims[position] // shards_of).reshape((-1,) + (1,) * (len(dims) - 1 - position))
    return gain


def gaussian(key, dims, spread, reach, cuts=(), dtype=jnp.bfloat16):
    level = levels(key, dims, cuts, -0.22, 0.18) if cuts else 1.0
    drawn = jax.random.normal(key, dims, jnp.float32) * spread * level
    return jnp.minimum(jnp.maximum(drawn, -reach), reach).astype(dtype)


def setup_inputs(seed: int = 0) -> dict:
    splits = jax.random.split(jax.random.key(seed), 7)
    volume = gaussian(splits[0], (C, NX, NY, NZ), 1.0, 6.0, ((0, 8), (1, 32)))
    weight_one = gaussian(splits[1], (C, C, 3, 3, 3), (C * 27) ** -0.5, 0.15625, ((0, 8),))
    bias_one = jnp.clip(jax.random.uniform(splits[2], (C,), jnp.float32, -0.5, 0.5) * levels(splits[2], (C,), ((0, 8),), -0.4, 0.0), -0.5, 0.5)
    weight_two = gaussian(splits[3], (C, C, 3, 3, 3), (C * 27) ** -0.5, 0.15625, ((0, 8),))
    bias_two = jnp.clip(jax.random.uniform(splits[4], (C,), jnp.float32, -0.5, 0.5) * levels(splits[4], (C,), ((0, 8),), -0.4, 0.0), -0.5, 0.5)
    cotangent = gaussian(splits[5], (C, NX, NY, NZ), 1.0, 6.0, ((0, 8), (1, 32)))
    return dict(volume=volume, weight_one=weight_one, bias_one=bias_one, weight_two=weight_two, bias_two=bias_two, cotangent=cotangent)


SLOPE = 0.2

def conv_same(inputs, kernel):
    return lax.conv_general_dilated(inputs.astype(jnp.float32)[None], kernel.astype(jnp.float32), (1, 1, 1), ((1, 1), (1, 1), (1, 1)), dimension_numbers=('NCDHW', 'OIDHW', 'NCDHW'), precision=lax.Precision.HIGHEST, preferred_element_type=jnp.float32)[0]

def conv_back(delta, kernel):
    flipped = jnp.flip(kernel.astype(jnp.float32), (2, 3, 4))
    return lax.conv_general_dilated(delta.astype(jnp.float32)[None], flipped, (1, 1, 1), ((1, 1), (1, 1), (1, 1)), dimension_numbers=('NCDHW', 'IODHW', 'NCDHW'), precision=lax.Precision.HIGHEST, preferred_element_type=jnp.float32)[0]

def kernel_grad(inputs, delta):
    padded = jnp.pad(inputs.astype(jnp.float32), ((0, 0), (1, 1), (1, 1), (1, 1)))
    result = lax.conv_general_dilated(padded[None], delta.astype(jnp.float32)[None], (1, 1, 1), ((0, 0), (0, 0), (0, 0)), dimension_numbers=('CNDHW', 'IODHW', 'NCDHW'), precision=lax.Precision.HIGHEST, preferred_element_type=jnp.float32)
    return jnp.transpose(result, (1, 0, 2, 3, 4))

def leaky(values):
    return jnp.where(values > 0, values, SLOPE * values)

def reference(volume, weight_one, bias_one, weight_two, bias_two, cotangent):
    pre_one = conv_same(volume, weight_one) + bias_one[:, None, None, None]
    act_one = leaky(pre_one).astype(jnp.bfloat16)
    pre_two = conv_same(act_one, weight_two) + bias_two[:, None, None, None]
    features = leaky(pre_two).astype(jnp.bfloat16)
    delta_two = (cotangent.astype(jnp.float32) * jnp.where(pre_two > 0, 1.0, SLOPE)).astype(jnp.bfloat16)
    scale = (NX * NY * NZ) ** (-0.5)
    grad_w_two = kernel_grad(act_one, delta_two) * scale
    grad_b_two = lax.optimization_barrier(jnp.sum(delta_two.astype(jnp.float32), axis=(1, 2, 3))) * scale
    back_one = conv_back(delta_two, weight_two)
    delta_one = (back_one * jnp.where(pre_one > 0, 1.0, SLOPE)).astype(jnp.bfloat16)
    grad_w_one = kernel_grad(volume, delta_one) * scale
    grad_b_one = lax.optimization_barrier(jnp.sum(delta_one.astype(jnp.float32), axis=(1, 2, 3))) * scale
    return (features, grad_w_one, grad_b_one, grad_w_two, grad_b_two)
```

```python
import jax
import jax.numpy as jnp
from jax import lax
from jax.experimental import pallas as pl
from jax.experimental.pallas import tpu as pltpu
from jax.sharding import Mesh, PartitionSpec as P

SLOPE = 0.2
F32 = jnp.float32
BF16 = jnp.bfloat16
SPACE = ("x", "h", "y")
PLANE = ("x", "y")
CHAN = ("l", "c")
CONTRACT_LAST = (((1,), (1,)), ((), ()))
VMEM_LIMIT = 48 * 1024 * 1024


def leaky(value):
    return jnp.where(value > 0, value, SLOPE * value)


def lanes(shape):
    return lax.broadcasted_iota(jnp.int32, shape, 1)


def tile(index, count=1):
    return pl.ds(pl.multiple_of(index * 128, 128), count * 128)


def along_y(array, step):
    y = lanes(array.shape) % 32
    edge = 0 if step == 1 else 31
    moved = pltpu.roll(array, step % array.shape[1], 1)
    return jnp.where(y == edge, 0.0, moved)


def add_y_taps(product):
    width = product.shape[1]
    split = product.reshape(8, 3, 8, width)
    below, middle, above = (split[:, k].reshape(64, width) for k in range(3))
    return middle + along_y(below, 1) + along_y(above, -1)


def stack_y(delta):
    parts = [along_y(delta, -1), delta, along_y(delta, 1)]
    parts = [part.reshape(8, 1, 8, part.shape[1]) for part in parts]
    return jnp.concatenate(parts, axis=1).reshape(192, delta.shape[1]).astype(BF16)


def stack_x(act):
    return (
        pltpu.roll(act, 32, 1).astype(BF16),
        act.astype(BF16),
        pltpu.roll(act, 96, 1).astype(BF16),
    )


def prepare_kernel(volume, cotangent, out, turned):
    turned[...] = jnp.zeros_like(turned)
    for ch in range(8):
        both = jnp.concatenate([volume[ch], cotangent[ch]], axis=0).astype(F32)
        turned[pl.ds(24 + ch, 128, stride=8), :] = both.T
    for block in range(8):
        out[block] = turned[pl.ds(block * 128, 176), :].astype(BF16)


def unpack_kernel(received, field, packed):
    low = lanes((64, 128)) < 64

    def body(j, carry):
        rows = pl.ds(pl.multiple_of(j * 16, 16), 16)
        pieces = [received[src, rows, :].astype(F32) for src in range(8)]
        even = jnp.concatenate([piece[:8] for piece in pieces], axis=0)
        odd = jnp.concatenate([piece[8:] for piece in pieces], axis=0)
        field[2 * j] = even.astype(BF16)
        field[2 * j + 1] = odd.astype(BF16)
        packed[j] = jnp.where(low, even, pltpu.roll(odd, 64, 1)).astype(BF16)
        return carry

    lax.fori_loop(0, 11, body, 0)


def forward_kernel(place, field, before, after, weights, act, wide, delta, feats, to_prev, to_next, pre, bias):
    lane = lanes((64, 128))

    def widen(j, carry):
        p = before[j].astype(F32)
        n = after[j].astype(F32)
        for half in range(2):
            row = 2 * j + half
            own = field[row].astype(F32)
            low = p if half == 0 else pltpu.roll(p, 64, 1)
            high = pltpu.roll(n, 64, 1) if half == 0 else n
            minus = jnp.where(lane < 64, low, pltpu.roll(own, 64, 1))
            plus = jnp.where(lane < 64, own, high)
            zero = jnp.where(lane < 32, pltpu.roll(minus, 96, 1), pltpu.roll(plus, 32, 1))
            wide[0:64, tile(row)] = minus.astype(BF16)
            wide[64:128, tile(row)] = zero.astype(BF16)
            wide[128:192, tile(row)] = plus.astype(BF16)
        return carry

    lax.fori_loop(0, 11, widen, 0)

    extra = weights[:, 1152:1280].astype(F32).reshape(8, 3, 8, 128)[:, 0].reshape(64, 128)
    for layer in range(2):
        parts = [extra[:, 3 * layer + k : 3 * layer + k + 1] for k in range(3)]
        bias[layer] = jnp.broadcast_to(parts[0] + parts[1] + parts[2], (64, 128))

    first, last = (place[0] == 0, place[0] == 31)
    outside = jnp.logical_or(
        jnp.logical_and(lane < 32, first), jnp.logical_and(lane >= 96, last)
    )

    def one(m, carry):
        product = sum(
            jnp.dot(
                weights[:, dz * 192 : dz * 192 + 192],
                wide[:, tile(2 * m + dz, 2)],
                preferred_element_type=F32,
            )
            for dz in range(3)
        )
        for half in range(2):
            row = 2 * m + half
            value = leaky(add_y_taps(product[:, half * 128 : half * 128 + 128]) + bias[0])
            z = place[1] * 16 + row - 2
            gone = jnp.logical_or(outside, jnp.logical_or(z < 0, z > 127))
            minus, zero, plus = stack_x(jnp.where(gone, 0.0, value))
            act[0:64, tile(row)] = minus
            act[64:128, tile(row)] = zero
            act[128:192, tile(row)] = plus
        return carry

    lax.fori_loop(0, 10, one, 0)

    own_lanes = jnp.logical_and(lane >= 32, lane < 96)

    def two(m, carry):
        product = sum(
            jnp.dot(
                weights[:, 576 + dz * 192 : 768 + dz * 192],
                act[:, tile(2 * m + dz, 2)],
                preferred_element_type=F32,
            )
            for dz in range(3)
        )
        for half in range(2):
            row = 2 * m + half
            value = add_y_taps(product[:, half * 128 : half * 128 + 128]) + bias[1]
            cot = pltpu.roll(field[row + 2].astype(F32), 96, 1)
            grad = jnp.where(value > 0, cot, SLOPE * cot)
            delta[row] = jnp.where(own_lanes, grad, 0.0).astype(BF16)
            pre[row] = leaky(value)
        return carry

    lax.fori_loop(0, 9, two, 0)

    for z in range(8):
        low = pltpu.roll(pre[z + 1], 96, 1)
        high = pltpu.roll(pre[z + 9], 32, 1)
        feats[z] = jnp.where(lane < 64, low, high).astype(BF16)

    for g in range(5):
        left = jnp.zeros((64, 128), F32)
        right = jnp.zeros((64, 128), F32)
        for i in range(4):
            if g + 5 * i < 18:
                row = delta[g + 5 * i].astype(F32)
                here = jnp.logical_and(lane >= 32 * i, lane < 32 * i + 32)
                left = jnp.where(here, pltpu.roll(row, (32 * i - 32) % 128, 1), left)
                right = jnp.where(here, pltpu.roll(row, (32 * i - 64) % 128, 1), right)
        to_prev[g] = left.astype(BF16)
        to_next[g] = right.astype(BF16)


def kernel_grad(stacked, wide, start, total, out, column):
    for dz in range(3):
        product = lax.dot_general(
            stacked[...],
            wide[:, (start + dz) * 128 : (start + dz) * 128 + 2048],
            CONTRACT_LAST,
            preferred_element_type=F32,
        )
        out[:, column + dz * 192 : column + dz * 192 + 192] = product.astype(BF16)
    summed = jnp.broadcast_to(jnp.sum(total, axis=1, keepdims=True), (64, 64))
    rows = jnp.broadcast_to(summed.reshape(8, 1, 8, 64), (8, 3, 8, 64)).reshape(192, 64)
    out[:, column + 576 : column + 640] = rows.astype(BF16)


def second_grad_kernel(delta, act, out, stacked):
    def body(z, total):
        value = delta[z + 1].astype(F32)
        stacked[:, tile(z)] = stack_y(value)
        return total + value

    total = lax.fori_loop(0, 16, body, jnp.zeros((64, 128), F32))
    kernel_grad(stacked, act, 1, total, out, 0)


def backward_kernel(delta, from_prev, from_next, weights, act, wide, grad_two, out, turned, stacked, own):
    lane = lanes((64, 128))
    for k in range(9):
        block = weights[:, 576 + 64 * k : 640 + 64 * k].astype(F32)
        turned[64 * k : 64 * k + 64, :] = block.T.astype(BF16)

    for row in range(18):
        g, i = (row % 5, row // 5)
        left = pltpu.roll(from_prev[g].astype(F32), (-32 * i) % 128, 1)
        right = pltpu.roll(from_next[g].astype(F32), (96 - 32 * i) % 128, 1)
        value = jnp.where(lane < 32, left, jnp.where(lane >= 96, right, delta[row].astype(F32)))
        stacked[:, row * 128 : row * 128 + 128] = stack_y(value)

    own_lanes = jnp.logical_and(lane >= 32, lane < 96)

    def body(m, total):
        product = sum(
            jnp.dot(
                turned[dz * 192 : dz * 192 + 192, :],
                stacked[:, tile(2 * m + 2 - dz, 2)],
                preferred_element_type=F32,
            )
            for dz in range(3)
        )
        for half in range(2):
            part = product[:, half * 128 : half * 128 + 128]
            back = part[64:128] + pltpu.roll(part[0:64], 96, 1) + pltpu.roll(part[128:192], 32, 1)
            positive = act[64:128, tile(2 * m + 2 + half)].astype(F32) > 0
            value = jnp.where(positive, back, SLOPE * back)
            value = jnp.where(own_lanes, value, 0.0).astype(BF16).astype(F32)
            own[:, tile(2 * m + half)] = stack_y(value)
            total = total + value
        return total

    total = lax.fori_loop(0, 8, body, jnp.zeros((64, 128), F32))
    out[:, 0:640] = grad_two[...]
    kernel_grad(own, wide, 2, total, out, 640)


def call(kernel, out_shapes, scratch, *args, scalars=0, flops=0):
    vmem = pl.BlockSpec(memory_space=pltpu.VMEM)
    smem = pl.BlockSpec(memory_space=pltpu.SMEM)
    outs = [jax.ShapeDtypeStruct(shape, dtype) for shape, dtype in out_shapes]
    size = sum(a.size * a.dtype.itemsize for a in args)
    size += sum(o.size * o.dtype.itemsize for o in outs)
    return pl.pallas_call(
        kernel,
        out_shape=outs,
        in_specs=[smem] * scalars + [vmem] * (len(args) - scalars),
        out_specs=[vmem] * len(outs),
        scratch_shapes=[pltpu.VMEM(shape, dtype) for shape, dtype in scratch],
        compiler_params=pltpu.CompilerParams(vmem_limit_bytes=VMEM_LIMIT),
        cost_estimate=pl.CostEstimate(flops=flops, bytes_accessed=size, transcendentals=0),
    )(*args)


def weight_rows(kernel):
    return jnp.transpose(kernel, (3, 0, 4, 2, 1)).reshape(24, 576)


def three_parts(bias):
    high = lax.reduce_precision(bias, 8, 7)
    middle = lax.reduce_precision(bias - high, 8, 7)
    low = bias - high - middle
    return [high, middle, low]


def restore(rows, column, factor):
    kernel = rows[:, column : column + 576].reshape(3, 8, 3, 3, 64)
    return (
        jnp.transpose(kernel, (1, 4, 3, 0, 2)) * factor,
        rows[0:8, column + 576] * factor,
    )


def shards(volume, weight_one, bias_one, weight_two, bias_two, cotangent):
    factor = float(volume.shape[1] * 32 * volume.shape[2] * volume.shape[3]) ** (-0.5)
    s, c = (lax.axis_index(SPACE), lax.axis_index(CHAN))
    up = [(i, i + 1) for i in range(31)]
    down = [(i + 1, i) for i in range(31)]

    offsets = jnp.stack(three_parts(bias_one) + three_parts(bias_two), axis=1)
    offsets = jnp.pad(offsets, ((0, 16), (0, 122))).astype(BF16)
    local = jnp.concatenate([weight_rows(weight_one), weight_rows(weight_two), offsets], axis=1)
    weights = lax.all_gather(local, CHAN, axis=0, tiled=True)

    (pieces,) = call(
        prepare_kernel,
        [((8, 176, 128), BF16)],
        [((1072, 128), F32)],
        volume.reshape(8, 64, 128),
        cotangent.reshape(8, 64, 128),
    )
    received = lax.all_to_all(pieces, CHAN, 0, 0)
    field, packed = call(
        unpack_kernel, [((22, 64, 128), BF16), ((11, 64, 128), BF16)], [], received
    )
    before = lax.ppermute(packed, SPACE, up)
    after = lax.ppermute(packed, SPACE, down)

    place = jnp.stack([s, c]).astype(jnp.int32)
    act, wide, delta, feats, to_prev, to_next = call(
        forward_kernel,
        [
            ((192, 2560), BF16),
            ((192, 2816), BF16),
            ((18, 64, 128), BF16),
            ((8, 64, 128), BF16),
            ((5, 64, 128), BF16),
            ((5, 64, 128), BF16),
        ],
        [((18, 64, 128), F32), ((2, 64, 128), F32)],
        place,
        field,
        before,
        after,
        weights,
        scalars=1,
        flops=2 * 192 * 576 * 128 * 38,
    )
    from_next = lax.ppermute(to_prev, SPACE, down)
    from_prev = lax.ppermute(to_next, SPACE, up)
    (grad_two,) = call(
        second_grad_kernel,
        [((192, 640), BF16)],
        [((192, 2048), BF16)],
        delta,
        act,
        flops=2 * 192 * 576 * 2048,
    )
    (grads,) = call(
        backward_kernel,
        [((192, 1280), BF16)],
        [((576, 192), BF16), ((192, 2304), BF16), ((192, 2048), BF16)],
        delta,
        from_prev,
        from_next,
        weights,
        act,
        wide,
        grad_two,
        flops=4 * 192 * 576 * 2048,
    )

    shares = lax.all_to_all(grads.reshape(8, 24, 1280), CHAN, 0, 0)
    mine = jnp.sum(shares.astype(F32), axis=0)
    mine = jnp.pad(mine.reshape(240, 128), ((0, 16), (0, 0))).reshape(16, 16, 128)
    shares = lax.all_to_all(mine, PLANE, 0, 0)
    part = jnp.sum(shares, axis=0)
    part = part + lax.ppermute(part, "h", [(0, 1), (1, 0)])
    whole = lax.all_to_all(jnp.broadcast_to(part, (16, 16, 128)), PLANE, 0, 0)
    rows = whole.reshape(256, 128)[:240].reshape(24, 1280)
    kernel_two, offset_two = restore(rows, 0, factor)
    kernel_one, offset_one = restore(rows, 640, factor)

    feats = jnp.transpose(feats.reshape(8, 8, 8, 128), (1, 0, 2, 3))
    feats = lax.all_to_all(feats, CHAN, 0, 0)
    feats = feats.reshape(8, 8, 8, 2, 2, 32)
    features = jnp.transpose(feats, (2, 4, 5, 0, 3, 1)).reshape(8, 2, 32, 128)
    return features, kernel_one, offset_one, kernel_two, offset_two


def solution(mesh):
    fine = Mesh(mesh.devices.reshape(4, 2, 4, 4, 2), ("x", "h", "y", "l", "c"))
    field = P(CHAN, SPACE, None, None)
    kernel = P(CHAN, None, None, None, None)
    in_specs = (field, kernel, P(CHAN), kernel, P(CHAN), field)
    out_specs = (field, kernel, P(CHAN), kernel, P(CHAN))
    return jax.shard_map(shards, mesh=fine, in_specs=in_specs, out_specs=out_specs, check_vma=False)
```

```python
import functools

import jax
import jax.numpy as jnp
from jax import lax
from jax.experimental import pallas as pl
from jax.experimental.pallas import tpu as pltpu
from jax.sharding import Mesh, PartitionSpec as P

SLOPE = 0.2
F32 = jnp.float32
BF16 = jnp.bfloat16
SPACE = ("x", "h", "y")
PLANE = ("x", "y")
CHAN = ("l", "c")
CONTRACT_LAST = (((1,), (1,)), ((), ()))
VMEM_LIMIT = 48 * 1024 * 1024


def leaky(value):
    return jnp.maximum(value, SLOPE * value)


def lanes(shape):
    return lax.broadcasted_iota(jnp.int32, shape, 1)


def tiles(index, count=1):
    return slice(index * 128, (index + count) * 128)


def along_y(array, step):
    y = lanes(array.shape) % 32
    edge = 0 if step == 1 else 31
    moved = pltpu.roll(array, step % array.shape[1], 1)
    return jnp.where(y == edge, 0.0, moved)


def add_y_taps(product):
    width = product.shape[1]
    split = product.reshape(8, 3, 8, width)
    below, middle, above = (split[:, k].reshape(64, width) for k in range(3))
    return middle + along_y(below, 1) + along_y(above, -1)


def stack_y(delta):
    parts = [along_y(delta, -1), delta, along_y(delta, 1)]
    parts = [part.reshape(8, 1, 8, part.shape[1]) for part in parts]
    return jnp.concatenate(parts, axis=1).reshape(192, delta.shape[1]).astype(BF16)


def conv_tiles(weights, column, stacked, start):
    return sum(
        jnp.dot(
            weights[:, column + dz * 192 : column + dz * 192 + 192],
            stacked[:, tiles(start + dz, 2)],
            preferred_element_type=F32,
        )
        for dz in range(3)
    )


def weight_prepare_kernel(weight_one, bias_one, weight_two, bias_two, units):
    row = lax.broadcasted_iota(jnp.int32, (8, 128), 0)
    lane = lanes((8, 128))

    rows = []
    for t in range(9):
        for dy in range(3):
            halves = []
            for half in range(2):
                layer, k = divmod(2 * t + half, 9)
                dz, dx = divmod(k, 3)
                halves.append((weight_two if layer else weight_one)[dx * 9 + dy * 3 + dz].astype(F32))
            rows.append(jnp.concatenate(halves, axis=1))
    packed = jnp.zeros((8, 128), F32)
    for layer, bias in enumerate((bias_one, bias_two)):
        value = sum(jnp.where(row == o, bias[o], 0.0) for o in range(8))
        for part in range(3):
            rounded = value.astype(BF16).astype(F32)
            packed = jnp.where(lane == 3 * layer + part, rounded, packed)
            value = value - rounded
    rows.append(packed)
    units[...] = jnp.concatenate(rows, axis=0).astype(BF16)


def prepare_kernel(place, volume, cotangent, out, held, turned, arrived):
    copies = [
        pltpu.make_async_copy(ref, held.at[k], arrived.at[k])
        for k, ref in enumerate((volume, cotangent))
    ]
    for copy in copies:
        copy.start()
    low = lanes((88, 128)) < 64
    turned[0:24] = jnp.zeros((24, 128), F32)
    turned[1048:1072] = jnp.zeros((24, 128), F32)
    for copy in copies:
        copy.wait()
    for ch in range(8):
        both = jnp.concatenate([held[0, ch], held[1, ch]], axis=0).astype(F32)
        turned[pl.ds(24 + ch, 128, stride=8), :] = both.T
    for block in range(8):
        target = jnp.where(place[3] == 1, 6 - 2 * (block // 2) + block % 2, block)
        rows = turned[block * 128 : block * 128 + 176].reshape(11, 2, 8, 128)
        even, odd = (rows[:, k].reshape(88, 128) for k in range(2))
        field = jnp.where(low, even, pltpu.roll(odd, 64, 1))
        left = turned[block * 128 + 16 : block * 128 + 96]
        right = turned[block * 128 + 80 : block * 128 + 160]
        cots = jnp.where(low[:80], pltpu.roll(left, 64, 1), right)
        out[target] = jnp.concatenate([field, cots], axis=0).astype(BF16)


def unpack_kernel(received, field, cots):
    pieces = [received[src].astype(F32) for src in range(8)]
    for j in range(21):
        both = jnp.concatenate([piece[8 * j : 8 * j + 8] for piece in pieces], axis=0).astype(BF16)
        if j < 11:
            field[j] = both
        else:
            cots[j - 11] = both


def weights_kernel(place, mine, other, out, back, bias):
    first = place[2] == 0
    for k in range(4):
        group = lax.rem(place[4] + 4 - k, 4)
        ours, theirs = (ref[k].astype(F32) for ref in (mine, other))
        pair = (jnp.where(first, ours, theirs), jnp.where(first, theirs, ours))
        rows = pl.ds(pl.multiple_of(48 * group, 16), 48)
        for t in range(9):
            block = jnp.concatenate([x[24 * t : 24 * t + 24] for x in pair], axis=0)
            out[rows, tiles(t)] = block.astype(BF16)
        extra = jnp.concatenate([x[216:224] for x in pair], axis=0)
        rows = pl.ds(pl.multiple_of(16 * group, 16), 16)
        for layer in range(2):
            parts = [extra[:, 3 * layer + k : 3 * layer + k + 1] for k in range(3)]
            bias[layer, rows] = jnp.broadcast_to(parts[0] + parts[1] + parts[2], (16, 128))
    kernel = out[:, 576:1152].astype(F32).reshape(8, 3, 8, 576)
    turned = [kernel[:, 2 - e].reshape(64, 576).T for e in range(3)]
    for column in range(9):
        block = [part[64 * (8 - column) : 64 * (8 - column) + 64].reshape(8, 1, 8, 64) for part in turned]
        block = jnp.concatenate(block, axis=1).reshape(192, 64)
        back[:, 64 * column : 64 * column + 64] = block.astype(BF16)


def forward_kernel(
    place, own, before, after, cotangent, weights, bias, act, wide, delta, feats, to_prev, to_next, post
):
    lane = lanes((64, 128))
    low = lane < 64

    for j in range(11):
        p, o, n = (ref[j].astype(F32) for ref in (before, own, after))
        turned = pltpu.roll(o, 64, 1)
        for half in range(2):
            if half == 0:
                minus = jnp.where(low, p, turned)
                plus = jnp.where(low, o, pltpu.roll(n, 64, 1))
            else:
                minus = jnp.where(low, pltpu.roll(p, 64, 1), o)
                plus = jnp.where(low, turned, n)
            zero = jnp.where(lane < 32, pltpu.roll(minus, 96, 1), pltpu.roll(plus, 32, 1))
            wide[0:64, tiles(2 * j + half)] = minus.astype(BF16)
            wide[64:128, tiles(2 * j + half)] = zero.astype(BF16)
            wide[128:192, tiles(2 * j + half)] = plus.astype(BF16)

    outside = jnp.logical_or(
        jnp.logical_and(lane < 32, place[0] == 0), jnp.logical_and(lane >= 96, place[0] == 31)
    )
    for m in range(10):
        product = conv_tiles(weights, 0, wide, 2 * m)
        for half in range(2):
            row = 2 * m + half
            value = leaky(add_y_taps(product[:, tiles(half)]) + bias[0])
            gone = outside
            if row < 2:
                gone = jnp.logical_or(outside, place[1] == 0)
            if row >= 18:
                gone = jnp.logical_or(outside, place[1] == 7)
            value = jnp.where(gone, 0.0, value)
            swapped = pltpu.roll(value, 64, 1).astype(BF16)
            if row < 12:
                left = slice(row * 128, row * 128 + 64)
                act[0:64, left] = value.astype(BF16)[:, 0:64]
                act[64:128, left] = pltpu.roll(value, 96, 1).astype(BF16)[:, 0:64]
                act[128:192, left] = swapped[:, 0:64]
            if row >= 8:
                right = slice((row - 8) * 128 + 64, (row - 8) * 128 + 128)
                act[0:64, right] = swapped[:, 64:128]
                act[64:128, right] = pltpu.roll(value, 32, 1).astype(BF16)[:, 64:128]
                act[128:192, right] = value.astype(BF16)[:, 64:128]

    front = lane % 64 < 32
    for m in range(5):
        product = conv_tiles(weights, 576, act, 2 * m)
        grads = []
        for half in range(2):
            row = 2 * m + half
            value = add_y_taps(product[:, tiles(half)]) + bias[1]
            cot = cotangent[row].astype(F32)
            grad = jnp.where(value > 0, cot, SLOPE * cot).astype(BF16)
            delta[row] = grad
            grads.append(grad.astype(F32))
            post[row] = leaky(value)
        to_prev[m] = jnp.where(front, grads[0], pltpu.roll(grads[1], 32, 1)).astype(BF16)
        to_next[m] = jnp.where(front, pltpu.roll(grads[0], 96, 1), grads[1]).astype(BF16)

    for block in range(8):
        turn = lax.rem(block // 2 + 4 - place[4], 4)
        same = jnp.where(place[2] == block % 2, 0, 1)
        piece = [post[z + 1, 8 * block : 8 * block + 8] for z in range(8)]
        feats[turn, same] = jnp.concatenate(piece, axis=0).astype(BF16)


def kernel_grad(stacked, wide, start):
    products = [
        lax.dot_general(
            stacked[...],
            wide[:, tiles(start + dz, 8)],
            CONTRACT_LAST,
            preferred_element_type=F32,
        )
        for dz in range(3)
    ]
    return jnp.concatenate(products, axis=1)


def second_grad_kernel(delta, act, wide, out, total, narrow, stacked):
    low = lanes((192, 128)) < 64
    for k in range(8):
        value = delta[k + 1].astype(F32)
        stacked[:, tiles(k)] = stack_y(value)
        total[...] = value if k == 0 else total[...] + value
    out[...] = kernel_grad(stacked, act, 1)
    for k in range(10):
        left = pltpu.roll(wide[:, tiles(k + 2)].astype(F32), 96, 1)
        right = pltpu.roll(wide[:, tiles(k + 10)].astype(F32), 32, 1)
        narrow[:, tiles(k)] = jnp.where(low, left, right).astype(BF16)


def backward_kernel(
    place, delta, from_prev, from_next, weights, act, narrow, grad_two, total_two, keep, send, stacked, own, both
):
    lane = lanes((64, 128))
    front = lane % 64 < 32
    for m in range(5):
        prev, after = (from_prev[m].astype(F32), from_next[m].astype(F32))
        for half in range(2):
            row = 2 * m + half
            value = delta[row].astype(F32)
            left = pltpu.roll(prev, 96, 1) if half else prev
            right = after if half else pltpu.roll(after, 32, 1)
            minus = jnp.where(front, left, pltpu.roll(value, 32, 1))
            plus = jnp.where(front, pltpu.roll(value, 96, 1), right)
            stacked[0:64, tiles(row)] = minus.astype(BF16)
            stacked[64:128, tiles(row)] = delta[row]
            stacked[128:192, tiles(row)] = plus.astype(BF16)

    total = jnp.zeros((64, 128), F32)
    for m in range(4):
        product = conv_tiles(weights, 0, stacked, 2 * m)
        for half in range(2):
            back = add_y_taps(product[:, tiles(half)])
            positive = act[64:128, tiles(2 * m + 2 + half)].astype(F32) > 0
            value = jnp.where(positive, back, SLOPE * back).astype(BF16).astype(F32)
            own[:, tiles(2 * m + half)] = stack_y(value)
            total = total + value

    both[:, 0:576] = grad_two[...]
    both[:, 576:1152] = kernel_grad(own, narrow, 0)
    offsets = jnp.where(
        lane == 0,
        jnp.sum(total_two[...], axis=1, keepdims=True),
        jnp.sum(total, axis=1, keepdims=True),
    )
    def block(index):
        rows = [both[24 * index + 8 * (u // 9) : 24 * index + 8 * (u // 9) + 8, tiles(u % 9)] for u in range(27)]
        return jnp.concatenate(rows + [offsets[8 * index : 8 * index + 8]], axis=0)

    first = place[2] == 0
    for group in range(4):
        even, odd = (block(2 * group), block(2 * group + 1))
        keep[group] = jnp.where(first, even, odd).astype(BF16)
        send[group] = jnp.where(first, odd, even).astype(BF16)


def finish_kernel(factor, whole, kernel_two, kernel_one, offsets):
    total = sum(whole[k].astype(F32) for k in range(16)) * factor
    units = [total[8 * u : 8 * u + 8] for u in range(28)]
    for dy in range(3):
        for column in range(9):
            value = units[dy * 9 + column]
            for half in range(2):
                layer, k = divmod(2 * column + half, 9)
                dz, dx = divmod(k, 3)
                target = kernel_one if layer else kernel_two
                target[dx * 9 + dy * 3 + dz] = value[:, 64 * half : 64 * half + 64]
    offsets[...] = units[27]


def features_kernel(place, *refs):
    pieces, other, out, turned = (refs[:4], refs[4], refs[5], refs[6])
    for k in range(4):
        group = lax.rem(place[4] + 4 - k, 4)
        group = jnp.where(place[3] == 1, 3 - group, group)
        for same in range(2):
            value = (pieces[k][0] if same == 0 else other[k]).astype(F32)
            core = place[2] if same == 0 else 1 - place[2]
            start = pl.multiple_of(128 * (2 * group + core), 128)
            turned[pl.ds(start, 64), :] = value
            turned[pl.ds(start + 64, 64), :] = pltpu.roll(value, 64, 1)
    for o in range(8):
        out[o] = turned[pl.ds(o, 128, stride=8), :].T[0:64].astype(BF16)


def call(kernel, out_shapes, scratch, *args, scalars=(), far=(), flops=0):
    vmem = pl.BlockSpec(memory_space=pltpu.VMEM)
    smem = pl.BlockSpec(memory_space=pltpu.SMEM)
    anywhere = pl.BlockSpec(memory_space=pl.ANY)
    outs = [jax.ShapeDtypeStruct(shape, dtype) for shape, dtype in out_shapes]
    size = sum(a.size * a.dtype.itemsize for a in args)
    size += sum(o.size * o.dtype.itemsize for o in outs)
    return pl.pallas_call(
        kernel,
        out_shape=outs,
        in_specs=[smem if k in scalars else anywhere if k in far else vmem for k in range(len(args))],
        out_specs=[vmem] * len(outs),
        scratch_shapes=[pltpu.VMEM(*x) if isinstance(x, tuple) else x for x in scratch],
        compiler_params=pltpu.CompilerParams(vmem_limit_bytes=VMEM_LIMIT),
        cost_estimate=pl.CostEstimate(flops=flops, bytes_accessed=size, transcendentals=0),
    )(*args)


def neighbours():
    pairs = []
    for here in range(31):
        there = here + 1
        turn = (here // 4) % 2 != (there // 4) % 2
        pairs += [(here * 4 + l, there * 4 + (3 - l if turn else l)) for l in range(4)]
    return pairs, [(b, a) for a, b in pairs]


def shards(volume, weight_one, bias_one, weight_two, bias_two, cotangent):
    factor = float(volume.shape[1] * 32 * volume.shape[2] * volume.shape[3]) ** (-0.5)
    h, l, c = (lax.axis_index(name) for name in ("h", "l", "c"))
    mirrored = h == 1
    block = 2 * jnp.where(mirrored, 3 - l, l) + c
    place = [lax.axis_index(SPACE), block, c, h, l]
    place = jnp.stack(place).astype(jnp.int32)
    up, down = neighbours()
    near = SPACE + ("l",)
    swap = [(0, 1), (1, 0)]

    def spread(pieces):
        turns = [[(i, (i + k) % 4) for i in range(4)] for k in range(4)]
        return [pieces[0]] + [lax.ppermute(pieces[k], "l", turns[k]) for k in range(1, 4)]

    (units,) = call(
        weight_prepare_kernel,
        [((224, 128), BF16)],
        [],
        jnp.transpose(weight_one, (2, 3, 4, 0, 1)).reshape(27, 8, 64),
        bias_one,
        jnp.transpose(weight_two, (2, 3, 4, 0, 1)).reshape(27, 8, 64),
        bias_two,
        scalars=(1, 3),
    )
    mine = jnp.stack(spread([units] * 4))
    other = lax.ppermute(mine, "c", swap)
    weights, weights_back, bias = call(
        weights_kernel,
        [((192, 1152), BF16), ((192, 576), BF16), ((2, 64, 128), F32)],
        [],
        place,
        mine,
        other,
        scalars=(0,),
    )

    (pieces,) = call(
        prepare_kernel,
        [((8, 168, 128), BF16)],
        [((2, 8, 64, 128), BF16), ((1072, 128), F32), pltpu.SemaphoreType.DMA((2,))],
        place,
        volume.reshape(8, 64, 128),
        cotangent.reshape(8, 64, 128),
        scalars=(0,),
        far=(1, 2),
    )
    received = lax.all_to_all(pieces, CHAN, 0, 0)
    field, cots = call(
        unpack_kernel, [((11, 64, 128), BF16), ((10, 64, 128), BF16)], [], received
    )
    before = lax.ppermute(field, near, up)
    after = lax.ppermute(field, near, down)

    act, wide, delta, feats, to_prev, to_next = call(
        forward_kernel,
        [
            ((192, 1536), BF16),
            ((192, 2816), BF16),
            ((10, 64, 128), BF16),
            ((4, 2, 64, 128), BF16),
            ((5, 64, 128), BF16),
            ((5, 64, 128), BF16),
        ],
        [((10, 64, 128), F32)],
        place,
        field,
        before,
        after,
        cots,
        weights,
        bias,
        scalars=(0,),
        flops=2 * 192 * 576 * 128 * 30,
    )
    from_next = lax.ppermute(to_prev, near, down)
    from_prev = lax.ppermute(to_next, near, up)
    grad_two, total_two, narrow = call(
        second_grad_kernel,
        [((192, 576), F32), ((64, 128), F32), ((192, 1280), BF16)],
        [((192, 1024), BF16)],
        delta,
        act,
        wide,
        flops=2 * 192 * 576 * 1024,
    )
    keep, send = call(
        backward_kernel,
        [((4, 224, 128), BF16), ((4, 224, 128), BF16)],
        [((192, 1280), BF16), ((192, 1024), BF16), ((192, 1152), F32)],
        place,
        delta,
        from_prev,
        from_next,
        weights_back,
        act,
        narrow,
        grad_two,
        total_two,
        scalars=(0,),
        flops=4 * 192 * 576 * 1024,
    )

    part = keep.astype(F32) + lax.ppermute(send, "c", swap).astype(F32)
    part = jnp.broadcast_to(part.astype(BF16)[None], (2, 4, 224, 128)).reshape(8, 224, 128)
    part = lax.all_to_all(part, ("h", "l"), 0, 0)
    part = jnp.sum(part.astype(F32), axis=0).astype(BF16)
    whole = lax.all_to_all(jnp.broadcast_to(part, (16, 224, 128)), PLANE, 0, 0)
    kernel_two, kernel_one, offsets = call(
        functools.partial(finish_kernel, factor),
        [((27, 8, 64), F32), ((27, 8, 64), F32), ((8, 128), F32)],
        [],
        whole,
    )
    kernel_one, kernel_two = (
        jnp.transpose(k.reshape(3, 3, 3, 8, 64), (3, 4, 0, 1, 2)) for k in (kernel_one, kernel_two)
    )

    feats = spread([feats[k] for k in range(4)])
    other = lax.ppermute(jnp.stack([piece[1] for piece in feats]), "c", swap)
    (features,) = call(
        features_kernel,
        [((8, 64, 128), BF16)],
        [((1024, 128), F32)],
        place,
        *feats,
        other,
        scalars=(0,),
    )
    return features.reshape(8, 2, 32, 128), kernel_one, offsets[:, 1], kernel_two, offsets[:, 0]


def solution(mesh):
    fine = Mesh(mesh.devices.reshape(4, 2, 4, 4, 2), ("x", "h", "y", "l", "c"))
    field = P(CHAN, SPACE, None, None)
    kernel = P(CHAN, None, None, None, None)
    in_specs = (field, kernel, P(CHAN), kernel, P(CHAN), field)
    out_specs = (field, kernel, P(CHAN), kernel, P(CHAN))
    return jax.shard_map(shards, mesh=fine, in_specs=in_specs, out_specs=out_specs, check_vma=False)
```

```python
import functools

import jax
import jax.numpy as jnp
from jax import lax
from jax.experimental import pallas as pl
from jax.experimental.pallas import tpu as pltpu
from jax.sharding import Mesh, PartitionSpec as P

SLOPE = 0.2
F32 = jnp.float32
BF16 = jnp.bfloat16
SPACE = ("x", "h", "y")
PLANE = ("x", "y")
CHAN = ("l", "c")
CONTRACT_LAST = (((1,), (1,)), ((), ()))
VMEM_LIMIT = 48 * 1024 * 1024


def leaky(value):
    return jnp.maximum(value, SLOPE * value)


def lanes(shape):
    return lax.broadcasted_iota(jnp.int32, shape, 1)


def tiles(index, count=1):
    return slice(index * 128, (index + count) * 128)


def along_y(array, step):
    y = lanes(array.shape) % 32
    edge = 0 if step == 1 else 31
    moved = pltpu.roll(array, step % array.shape[1], 1)
    return jnp.where(y == edge, 0.0, moved)


def add_y_taps(product):
    width = product.shape[1]
    split = product.reshape(8, 3, 8, width)
    below, middle, above = (split[:, k].reshape(64, width) for k in range(3))
    return middle + along_y(below, 1) + along_y(above, -1)


def stack_y(delta):
    parts = [along_y(delta, -1), delta, along_y(delta, 1)]
    parts = [part.reshape(8, 1, 8, part.shape[1]) for part in parts]
    return jnp.concatenate(parts, axis=1).reshape(192, delta.shape[1]).astype(BF16)


def conv_tiles(weights, column, stacked, start):
    return sum(
        jnp.dot(
            weights[:, column + dz * 192 : column + dz * 192 + 192],
            stacked[:, tiles(start + dz, 2)],
            preferred_element_type=F32,
        )
        for dz in range(3)
    )


def weight_prepare_kernel(weight_one, bias_one, weight_two, bias_two, units, held, arrived):
    copies = [
        pltpu.make_async_copy(ref, held.at[k], arrived.at[k])
        for k, ref in enumerate((weight_one, weight_two))
    ]
    for copy in copies:
        copy.start()
    row = lax.broadcasted_iota(jnp.int32, (8, 128), 0)
    lane = lanes((8, 128))

    for copy in copies:
        copy.wait()
    rows = []
    for t in range(9):
        for dy in range(3):
            halves = []
            for half in range(2):
                layer, k = divmod(2 * t + half, 9)
                dz, dx = divmod(k, 3)
                halves.append(held[layer, dx * 9 + dy * 3 + dz].astype(F32))
            rows.append(jnp.concatenate(halves, axis=1))
    packed = jnp.zeros((8, 128), F32)
    for layer, bias in enumerate((bias_one, bias_two)):
        value = sum(jnp.where(row == o, bias[o], 0.0) for o in range(8))
        for part in range(3):
            rounded = value.astype(BF16).astype(F32)
            packed = jnp.where(lane == 3 * layer + part, rounded, packed)
            value = value - rounded
    rows.append(packed)
    units[...] = jnp.concatenate(rows, axis=0).astype(BF16)


def prepare_kernel(place, volume, cotangent, out, held, turned, arrived):
    copies = [
        pltpu.make_async_copy(ref, held.at[k], arrived.at[k])
        for k, ref in enumerate((volume, cotangent))
    ]
    for copy in copies:
        copy.start()
    low = lanes((88, 128)) < 64
    turned[0:24] = jnp.zeros((24, 128), F32)
    turned[1048:1072] = jnp.zeros((24, 128), F32)
    for copy in copies:
        copy.wait()
    for ch in range(8):
        both = jnp.concatenate([held[0, ch], held[1, ch]], axis=0).astype(F32)
        turned[pl.ds(24 + ch, 128, stride=8), :] = both.T
    for block in range(8):
        target = jnp.where(place[3] == 1, 6 - 2 * (block // 2) + block % 2, block)
        rows = turned[block * 128 : block * 128 + 176].reshape(11, 2, 8, 128)
        even, odd = (rows[:, k].reshape(88, 128) for k in range(2))
        field = jnp.where(low, even, pltpu.roll(odd, 64, 1))
        left = turned[block * 128 + 16 : block * 128 + 96]
        right = turned[block * 128 + 80 : block * 128 + 160]
        cots = jnp.where(low[:80], pltpu.roll(left, 64, 1), right)
        out[target] = jnp.concatenate([field, cots], axis=0).astype(BF16)


def unpack_kernel(received, field, cots):
    pieces = [received[src].astype(F32) for src in range(8)]
    for j in range(21):
        both = jnp.concatenate([piece[8 * j : 8 * j + 8] for piece in pieces], axis=0).astype(BF16)
        if j < 11:
            field[j] = both
        else:
            cots[j - 11] = both


def weights_kernel(place, mine, other, out, back, bias):
    first = place[2] == 0
    for k in range(4):
        group = lax.rem(place[4] + 4 - k, 4)
        ours, theirs = (ref[k].astype(F32) for ref in (mine, other))
        pair = (jnp.where(first, ours, theirs), jnp.where(first, theirs, ours))
        rows = pl.ds(pl.multiple_of(48 * group, 16), 48)
        for t in range(9):
            block = jnp.concatenate([x[24 * t : 24 * t + 24] for x in pair], axis=0)
            out[rows, tiles(t)] = block.astype(BF16)
        extra = jnp.concatenate([x[216:224] for x in pair], axis=0)
        rows = pl.ds(pl.multiple_of(16 * group, 16), 16)
        for layer in range(2):
            parts = [extra[:, 3 * layer + k : 3 * layer + k + 1] for k in range(3)]
            bias[layer, rows] = jnp.broadcast_to(parts[0] + parts[1] + parts[2], (16, 128))
    kernel = out[:, 576:1152].astype(F32).reshape(8, 3, 8, 576)
    turned = [kernel[:, 2 - e].reshape(64, 576).T for e in range(3)]
    for column in range(9):
        block = [part[64 * (8 - column) : 64 * (8 - column) + 64].reshape(8, 1, 8, 64) for part in turned]
        block = jnp.concatenate(block, axis=1).reshape(192, 64)
        back[:, 64 * column : 64 * column + 64] = block.astype(BF16)


def forward_kernel(
    place, own, even, odd, cotangent, weights, bias, act, wide, delta, feats, to_even, to_odd, post
):
    upper = lax.rem(place[0], 2) == 1
    lane = lanes((64, 128))
    low = lane < 64

    for j in range(11):
        o, x, y = (ref[j].astype(F32) for ref in (own, even, odd))
        p, n = (jnp.where(upper, x, y), jnp.where(upper, y, x))
        turned = pltpu.roll(o, 64, 1)
        for half in range(2):
            if half == 0:
                minus = jnp.where(low, p, turned)
                plus = jnp.where(low, o, pltpu.roll(n, 64, 1))
            else:
                minus = jnp.where(low, pltpu.roll(p, 64, 1), o)
                plus = jnp.where(low, turned, n)
            zero = jnp.where(lane < 32, pltpu.roll(minus, 96, 1), pltpu.roll(plus, 32, 1))
            wide[0:64, tiles(2 * j + half)] = minus.astype(BF16)
            wide[64:128, tiles(2 * j + half)] = zero.astype(BF16)
            wide[128:192, tiles(2 * j + half)] = plus.astype(BF16)

    outside = jnp.logical_or(
        jnp.logical_and(lane < 32, place[0] == 0), jnp.logical_and(lane >= 96, place[0] == 31)
    )
    for m in range(10):
        product = conv_tiles(weights, 0, wide, 2 * m)
        for half in range(2):
            row = 2 * m + half
            value = leaky(add_y_taps(product[:, tiles(half)]) + bias[0])
            gone = outside
            if row < 2:
                gone = jnp.logical_or(outside, place[1] == 0)
            if row >= 18:
                gone = jnp.logical_or(outside, place[1] == 7)
            value = jnp.where(gone, 0.0, value)
            swapped = pltpu.roll(value, 64, 1).astype(BF16)
            if row < 12:
                left = slice(row * 128, row * 128 + 64)
                act[0:64, left] = value.astype(BF16)[:, 0:64]
                act[64:128, left] = pltpu.roll(value, 96, 1).astype(BF16)[:, 0:64]
                act[128:192, left] = swapped[:, 0:64]
            if row >= 8:
                right = slice((row - 8) * 128 + 64, (row - 8) * 128 + 128)
                act[0:64, right] = swapped[:, 64:128]
                act[64:128, right] = pltpu.roll(value, 32, 1).astype(BF16)[:, 64:128]
                act[128:192, right] = value.astype(BF16)[:, 64:128]

    front = lane % 64 < 32
    for m in range(5):
        product = conv_tiles(weights, 576, act, 2 * m)
        grads = []
        for half in range(2):
            row = 2 * m + half
            value = add_y_taps(product[:, tiles(half)]) + bias[1]
            cot = cotangent[row].astype(F32)
            grad = jnp.where(value > 0, cot, SLOPE * cot).astype(BF16)
            delta[row] = grad
            grads.append(grad.astype(F32))
            post[row] = leaky(value)
        to_prev = jnp.where(front, grads[0], pltpu.roll(grads[1], 32, 1))
        to_next = jnp.where(front, pltpu.roll(grads[0], 96, 1), grads[1])
        to_even[m] = jnp.where(upper, to_prev, to_next).astype(BF16)
        to_odd[m] = jnp.where(upper, to_next, to_prev).astype(BF16)

    for block in range(8):
        turn = lax.rem(block // 2 + 4 - place[4], 4)
        same = jnp.where(place[2] == block % 2, 0, 1)
        piece = [post[z + 1, 8 * block : 8 * block + 8] for z in range(8)]
        feats[turn, same] = jnp.concatenate(piece, axis=0).astype(BF16)


def kernel_grad(stacked, wide, start):
    products = [
        lax.dot_general(
            stacked[...],
            wide[:, tiles(start + dz, 8)],
            CONTRACT_LAST,
            preferred_element_type=F32,
        )
        for dz in range(3)
    ]
    return jnp.concatenate(products, axis=1)


def second_grad_kernel(delta, act, wide, out, total, narrow, stacked):
    low = lanes((192, 128)) < 64
    for k in range(8):
        value = delta[k + 1].astype(F32)
        stacked[:, tiles(k)] = stack_y(value)
        total[...] = value if k == 0 else total[...] + value
    out[...] = kernel_grad(stacked, act, 1)
    for k in range(10):
        left = pltpu.roll(wide[:, tiles(k + 2)].astype(F32), 96, 1)
        right = pltpu.roll(wide[:, tiles(k + 10)].astype(F32), 32, 1)
        narrow[:, tiles(k)] = jnp.where(low, left, right).astype(BF16)


def backward_kernel(
    place, delta, from_even, from_odd, weights, act, narrow, grad_two, total_two, keep, send, stacked, own, both
):
    lane = lanes((64, 128))
    upper = lax.rem(place[0], 2) == 1
    front = lane % 64 < 32
    for m in range(5):
        x, y = (from_even[m].astype(F32), from_odd[m].astype(F32))
        prev, after = (jnp.where(upper, x, y), jnp.where(upper, y, x))
        for half in range(2):
            row = 2 * m + half
            value = delta[row].astype(F32)
            left = pltpu.roll(prev, 96, 1) if half else prev
            right = after if half else pltpu.roll(after, 32, 1)
            minus = jnp.where(front, left, pltpu.roll(value, 32, 1))
            plus = jnp.where(front, pltpu.roll(value, 96, 1), right)
            stacked[0:64, tiles(row)] = minus.astype(BF16)
            stacked[64:128, tiles(row)] = delta[row]
            stacked[128:192, tiles(row)] = plus.astype(BF16)

    total = jnp.zeros((64, 128), F32)
    for m in range(4):
        product = conv_tiles(weights, 0, stacked, 2 * m)
        for half in range(2):
            back = add_y_taps(product[:, tiles(half)])
            positive = act[64:128, tiles(2 * m + 2 + half)].astype(F32) > 0
            value = jnp.where(positive, back, SLOPE * back).astype(BF16).astype(F32)
            own[:, tiles(2 * m + half)] = stack_y(value)
            total = total + value

    both[:, 0:576] = grad_two[...]
    both[:, 576:1152] = kernel_grad(own, narrow, 0)
    offsets = jnp.where(
        lane == 0,
        jnp.sum(total_two[...], axis=1, keepdims=True),
        jnp.sum(total, axis=1, keepdims=True),
    )
    def block(index):
        rows = [both[24 * index + 8 * (u // 9) : 24 * index + 8 * (u // 9) + 8, tiles(u % 9)] for u in range(27)]
        return jnp.concatenate(rows + [offsets[8 * index : 8 * index + 8]], axis=0)

    first = place[2] == 0
    for group in range(4):
        even, odd = (block(2 * group), block(2 * group + 1))
        turn = lax.rem(group + 4 - place[4], 4)
        keep[turn] = jnp.where(first, even, odd).astype(BF16)
        send[turn] = jnp.where(first, odd, even).astype(BF16)


def sum_of_four(parts):
    parts = [part.astype(F32) for part in parts]
    return (parts[0] + parts[2]) + (parts[1] + parts[3])


def finish_kernel(factor, first, second, third, fourth, kernel_two, kernel_one, offsets):
    total = sum_of_four([first[...], second[...], third[...], fourth[...]]) * factor
    units = [total[8 * u : 8 * u + 8] for u in range(28)]
    for dy in range(3):
        for column in range(9):
            value = units[dy * 9 + column]
            for half in range(2):
                layer, k = divmod(2 * column + half, 9)
                dz, dx = divmod(k, 3)
                target = kernel_one if layer else kernel_two
                target[dx * 9 + dy * 3 + dz] = value[:, 64 * half : 64 * half + 64]
    offsets[...] = units[27]


def features_kernel(place, *refs):
    pieces, other, out, turned = (refs[:4], refs[4], refs[5], refs[6])
    for k in range(4):
        group = lax.rem(place[4] + 4 - k, 4)
        group = jnp.where(place[3] == 1, 3 - group, group)
        for same in range(2):
            value = (pieces[k][0] if same == 0 else other[k]).astype(F32)
            core = place[2] if same == 0 else 1 - place[2]
            start = pl.multiple_of(128 * (2 * group + core), 128)
            turned[pl.ds(start, 64), :] = value
            turned[pl.ds(start + 64, 64), :] = pltpu.roll(value, 64, 1)
    for o in range(8):
        out[o] = turned[pl.ds(o, 128, stride=8), :].T[0:64].astype(BF16)


def call(kernel, out_shapes, scratch, *args, scalars=(), far=(), flops=0):
    vmem = pl.BlockSpec(memory_space=pltpu.VMEM)
    smem = pl.BlockSpec(memory_space=pltpu.SMEM)
    anywhere = pl.BlockSpec(memory_space=pl.ANY)
    outs = [jax.ShapeDtypeStruct(shape, dtype) for shape, dtype in out_shapes]
    size = sum(a.size * a.dtype.itemsize for a in args)
    size += sum(o.size * o.dtype.itemsize for o in outs)
    return pl.pallas_call(
        kernel,
        out_shape=outs,
        in_specs=[smem if k in scalars else anywhere if k in far else vmem for k in range(len(args))],
        out_specs=[vmem] * len(outs),
        scratch_shapes=[pltpu.VMEM(*x) if isinstance(x, tuple) else x for x in scratch],
        compiler_params=pltpu.CompilerParams(vmem_limit_bytes=VMEM_LIMIT),
        cost_estimate=pl.CostEstimate(flops=flops, bytes_accessed=size, transcendentals=0),
    )(*args)


def neighbours():
    both = []
    for start in range(2):
        pairs = []
        for here in range(start, 31, 2):
            there = here + 1
            turn = (here // 4) % 2 != (there // 4) % 2
            for l in range(4):
                pair = (here * 4 + l, there * 4 + (3 - l if turn else l))
                pairs += [pair, pair[::-1]]
        both.append(pairs)
    return both


def shards(volume, weight_one, bias_one, weight_two, bias_two, cotangent):
    factor = float(volume.shape[1] * 32 * volume.shape[2] * volume.shape[3]) ** (-0.5)
    h, l, c = (lax.axis_index(name) for name in ("h", "l", "c"))
    mirrored = h == 1
    block = 2 * jnp.where(mirrored, 3 - l, l) + c
    place = [lax.axis_index(SPACE), block, c, h, l]
    place = jnp.stack(place).astype(jnp.int32)
    even, odd = neighbours()
    near = SPACE + ("l",)
    swap = [(0, 1), (1, 0)]

    def spread(pieces, axis="l"):
        turns = [[(i, (i + k) % 4) for i in range(4)] for k in range(4)]
        return [pieces[0]] + [lax.ppermute(pieces[k], axis, turns[k]) for k in range(1, 4)]

    (units,) = call(
        weight_prepare_kernel,
        [((224, 128), BF16)],
        [((2, 27, 8, 64), BF16), pltpu.SemaphoreType.DMA((2,))],
        jnp.transpose(weight_one, (2, 3, 4, 0, 1)).reshape(27, 8, 64),
        bias_one,
        jnp.transpose(weight_two, (2, 3, 4, 0, 1)).reshape(27, 8, 64),
        bias_two,
        scalars=(1, 3),
        far=(0, 2),
    )
    mine = spread([units] * 4)

    (pieces,) = call(
        prepare_kernel,
        [((8, 168, 128), BF16)],
        [((2, 8, 64, 128), BF16), ((1072, 128), F32), pltpu.SemaphoreType.DMA((2,))],
        place,
        volume.reshape(8, 64, 128),
        cotangent.reshape(8, 64, 128),
        scalars=(0,),
        far=(1, 2),
    )
    received = lax.all_to_all(pieces, CHAN, 0, 0)
    field, cots = call(
        unpack_kernel, [((11, 64, 128), BF16), ((10, 64, 128), BF16)], [], received
    )
    near_even = lax.ppermute(field, near, even)
    near_odd = lax.ppermute(field, near, odd)
    mine, near_even = lax.optimization_barrier((mine, near_even))
    mine = jnp.stack(mine)
    other = lax.ppermute(mine, "c", swap)
    weights, weights_back, bias = call(
        weights_kernel,
        [((192, 1152), BF16), ((192, 576), BF16), ((2, 64, 128), F32)],
        [],
        place,
        mine,
        other,
        scalars=(0,),
    )

    act, wide, delta, feats, to_even, to_odd = call(
        forward_kernel,
        [
            ((192, 1536), BF16),
            ((192, 2816), BF16),
            ((10, 64, 128), BF16),
            ((4, 2, 64, 128), BF16),
            ((5, 64, 128), BF16),
            ((5, 64, 128), BF16),
        ],
        [((10, 64, 128), F32)],
        place,
        field,
        near_even,
        near_odd,
        cots,
        weights,
        bias,
        scalars=(0,),
        flops=2 * 192 * 576 * 128 * 30,
    )
    from_even = lax.ppermute(to_even, near, even)
    from_odd = lax.ppermute(to_odd, near, odd)
    grad_two, total_two, narrow = call(
        second_grad_kernel,
        [((192, 576), F32), ((64, 128), F32), ((192, 1280), BF16)],
        [((192, 1024), BF16)],
        delta,
        act,
        wide,
        flops=2 * 192 * 576 * 1024,
    )
    keep, send = call(
        backward_kernel,
        [((4, 224, 128), BF16), ((4, 224, 128), BF16)],
        [((192, 1280), BF16), ((192, 1024), BF16), ((192, 1152), F32)],
        place,
        delta,
        from_even,
        from_odd,
        weights_back,
        act,
        narrow,
        grad_two,
        total_two,
        scalars=(0,),
        flops=4 * 192 * 576 * 1024,
    )

    other = lax.ppermute(send, "c", swap)
    parts = [(keep[k].astype(F32) + other[k].astype(F32)).astype(BF16) for k in range(4)]
    part = sum_of_four(spread(parts)).astype(BF16)
    other = lax.ppermute(part, "h", swap)
    part = (part.astype(F32) + other.astype(F32)).astype(BF16)
    part = sum_of_four(spread([part] * 4, "y")).astype(BF16)
    parts = spread([part] * 4, "x")
    kernel_two, kernel_one, offsets = call(
        functools.partial(finish_kernel, factor),
        [((27, 8, 64), F32), ((27, 8, 64), F32), ((8, 128), F32)],
        [],
        *parts,
    )
    kernel_one, kernel_two = (
        jnp.transpose(k.reshape(3, 3, 3, 8, 64), (3, 4, 0, 1, 2)) for k in (kernel_one, kernel_two)
    )

    feats = spread([feats[k] for k in range(4)])
    other = lax.ppermute(jnp.stack([piece[1] for piece in feats]), "c", swap)
    (features,) = call(
        features_kernel,
        [((8, 64, 128), BF16)],
        [((1024, 128), F32)],
        place,
        *feats,
        other,
        scalars=(0,),
    )
    return features.reshape(8, 2, 32, 128), kernel_one, offsets[:, 1], kernel_two, offsets[:, 0]


def solution(mesh):
    fine = Mesh(mesh.devices.reshape(4, 2, 4, 4, 2), ("x", "h", "y", "l", "c"))
    field = P(CHAN, SPACE, None, None)
    kernel = P(CHAN, None, None, None, None)
    in_specs = (field, kernel, P(CHAN), kernel, P(CHAN), field)
    out_specs = (field, kernel, P(CHAN), kernel, P(CHAN))
    return jax.shard_map(shards, mesh=fine, in_specs=in_specs, out_specs=out_specs, check_vma=False)
```

```python
import functools

import jax
import jax.numpy as jnp
from jax import lax
from jax.experimental import pallas as pl
from jax.experimental.pallas import tpu as pltpu
from jax.sharding import Mesh, PartitionSpec as P

SLOPE = 0.2
F32 = jnp.float32
BF16 = jnp.bfloat16
SPACE = ("x", "h", "y")
PLANE = ("x", "y")
CHAN = ("l", "c")
CONTRACT_LAST = (((1,), (1,)), ((), ()))
VMEM_LIMIT = 48 * 1024 * 1024
FULL_LIMIT = 63 * 1024 * 1024


def leaky(value):
    return jnp.maximum(value, SLOPE * value)


def lanes(shape):
    return lax.broadcasted_iota(jnp.int32, shape, 1)


def tiles(index, count=1):
    return slice(index * 128, (index + count) * 128)


def along_y(array, step):
    y = lanes(array.shape) % 32
    edge = 0 if step == 1 else 31
    moved = pltpu.roll(array, step % array.shape[1], 1)
    return jnp.where(y == edge, 0.0, moved)


def add_y_taps(product):
    width = product.shape[1]
    split = product.reshape(8, 3, 8, width)
    below, middle, above = (split[:, k].reshape(64, width) for k in range(3))
    return middle + along_y(below, 1) + along_y(above, -1)


def stack_y(delta):
    parts = [along_y(delta, -1), delta, along_y(delta, 1)]
    parts = [part.reshape(8, 1, 8, part.shape[1]) for part in parts]
    return jnp.concatenate(parts, axis=1).reshape(192, delta.shape[1]).astype(BF16)


def conv_tiles(weights, column, stacked, start):
    return sum(
        jnp.dot(
            weights[:, column + dz * 192 : column + dz * 192 + 192],
            stacked[:, tiles(start + dz, 2)],
            preferred_element_type=F32,
        )
        for dz in range(3)
    )


def turn_field(place, held, turned):
    turned[0:24] = jnp.zeros((24, 128), F32)
    turned[1048:1072] = jnp.zeros((24, 128), F32)
    for ch in range(8):
        value = held[ch].astype(F32)
        turned[pl.ds(24 + ch, 128, stride=8), :] = jnp.concatenate([value, value], axis=0).T


def target_of(place, block):
    chip = jnp.where(place[3] == 1, 3 - block // 2, block // 2)
    return lax.rem(chip + 4 - place[4], 4), jnp.where(place[2] == block % 2, 0, 1)


def volume_kernel(place, volume, out, held, turned, arrived):
    copy = pltpu.make_async_copy(volume, held, arrived)
    copy.start()
    low = lanes((88, 128)) < 64
    copy.wait()
    turn_field(place, held, turned)
    for block in range(8):
        turn, same = target_of(place, block)
        rows = turned[block * 128 : block * 128 + 176].reshape(11, 2, 8, 128)
        even, odd = (rows[:, k].reshape(88, 128) for k in range(2))
        out[turn, same] = jnp.where(low, even, odd).astype(BF16)


def rest_kernel(
    place,
    cotangent,
    weight_one,
    bias_one,
    weight_two,
    bias_two,
    first,
    second,
    third,
    fourth,
    held,
    turned,
    kernels,
    biases,
    arrived,
):
    copies = [
        pltpu.make_async_copy(ref, to, arrived.at[k])
        for k, (ref, to) in enumerate(
            (
                (cotangent, held),
                (weight_one, kernels.at[0]),
                (weight_two, kernels.at[1]),
                (bias_one, biases.at[0]),
                (bias_two, biases.at[1]),
            )
        )
    ]
    for copy in copies:
        copy.start()
    for copy in copies:
        copy.wait()

    row = lax.broadcasted_iota(jnp.int32, (8, 128), 0)
    lane = lanes((8, 128))
    rows = []
    for t in range(9):
        for dy in range(3):
            halves = []
            for half in range(2):
                layer, k = divmod(2 * t + half, 9)
                dz, dx = divmod(k, 3)
                halves.append(kernels[layer, dx * 9 + dy * 3 + dz].astype(F32))
            rows.append(jnp.concatenate(halves, axis=1))
    packed = jnp.zeros((8, 128), F32)
    for layer in range(2):
        value = sum(jnp.where(row == o, biases[layer, o], 0.0) for o in range(8))
        for part in range(3):
            rounded = value.astype(BF16).astype(F32)
            packed = jnp.where(lane == 3 * layer + part, rounded, packed)
            value = value - rounded
    rows.append(packed)
    turn_field(place, held, turned)
    low = lanes((80, 128)) < 64
    for k, out in enumerate((first, second, third, fourth)):
        chip = lax.rem(place[4] + k, 4)
        chip = jnp.where(place[3] == 1, 3 - chip, chip)
        pieces = []
        for same in range(2):
            block = 2 * chip + (1 - place[2] if same else place[2])
            start = pl.multiple_of(block * 128, 128)
            pieces.append(jnp.where(low, turned[pl.ds(start + 16, 80)], turned[pl.ds(start + 80, 80)]))
        out[...] = jnp.concatenate(pieces + rows, axis=0).astype(BF16)


def channel_order(place, ours, theirs):
    first = place[2] == 0
    pieces = [None] * 8
    pairs = [(jnp.where(first, a, b), jnp.where(first, b, a)) for a, b in zip(ours, theirs)]
    for chip in range(4):
        turn = lax.rem(place[4] + 4 - chip, 4)
        for core in range(2):
            value = pairs[3][core]
            for k in range(3):
                value = jnp.where(turn == k, pairs[k][core], value)
            pieces[2 * chip + core] = value
    return pieces


def unpack_kernel(place, *refs):
    ours, theirs, field = (refs[:4], refs[4:8], refs[8])
    ours = [ref[0].astype(F32) for ref in ours]
    theirs = [ref[1].astype(F32) for ref in theirs]
    pieces = channel_order(place, ours, theirs)
    for j in range(11):
        both = jnp.concatenate([piece[8 * j : 8 * j + 8] for piece in pieces], axis=0)
        field[j] = both.astype(BF16)


def weights_kernel(place, *refs):
    ours, theirs = (refs[:4], refs[4:8])
    out, back, bias, cots = refs[8:]
    pieces = channel_order(
        place, [ref[0:80].astype(F32) for ref in ours], [ref[80:160].astype(F32) for ref in theirs]
    )
    for j in range(10):
        both = jnp.concatenate([piece[8 * j : 8 * j + 8] for piece in pieces], axis=0)
        cots[j] = both.astype(BF16)

    first = place[2] == 0
    for k in range(4):
        group = lax.rem(place[4] + 4 - k, 4)
        mine, other = (ref[160:384].astype(F32) for ref in (ours[k], theirs[k]))
        pair = (jnp.where(first, mine, other), jnp.where(first, other, mine))
        rows = pl.ds(pl.multiple_of(48 * group, 16), 48)
        for t in range(9):
            block = jnp.concatenate([x[24 * t : 24 * t + 24] for x in pair], axis=0)
            out[rows, tiles(t)] = block.astype(BF16)
        extra = jnp.concatenate([x[216:224] for x in pair], axis=0)
        rows = pl.ds(pl.multiple_of(16 * group, 16), 16)
        for layer in range(2):
            parts = [extra[:, 3 * layer + k : 3 * layer + k + 1] for k in range(3)]
            bias[layer, rows] = jnp.broadcast_to(parts[0] + parts[1] + parts[2], (16, 128))
    kernel = out[:, 576:1152].astype(F32).reshape(8, 3, 8, 576)
    turned = [kernel[:, 2 - e].reshape(64, 576).T for e in range(3)]
    for column in range(9):
        block = [part[64 * (8 - column) : 64 * (8 - column) + 64].reshape(8, 1, 8, 64) for part in turned]
        block = jnp.concatenate(block, axis=1).reshape(192, 64)
        back[:, 64 * column : 64 * column + 64] = block.astype(BF16)


def forward_kernel(
    place, own, even, odd, cotangent, weights, bias, act, wide, delta, feats, to_even, to_odd, post
):
    upper = lax.rem(place[0], 2) == 1
    lane = lanes((64, 128))
    low = lane < 64

    for j in range(11):
        o, x, y = (ref[j].astype(F32) for ref in (own, even, odd))
        p, n = (jnp.where(upper, x, y), jnp.where(upper, y, x))
        turned = pltpu.roll(o, 64, 1)
        for half in range(2):
            if half == 0:
                minus = jnp.where(low, p, turned)
                plus = jnp.where(low, o, pltpu.roll(n, 64, 1))
            else:
                minus = jnp.where(low, pltpu.roll(p, 64, 1), o)
                plus = jnp.where(low, turned, n)
            zero = jnp.where(lane < 32, pltpu.roll(minus, 96, 1), pltpu.roll(plus, 32, 1))
            wide[0:64, tiles(2 * j + half)] = minus.astype(BF16)
            wide[64:128, tiles(2 * j + half)] = zero.astype(BF16)
            wide[128:192, tiles(2 * j + half)] = plus.astype(BF16)

    outside = jnp.logical_or(
        jnp.logical_and(lane < 32, place[0] == 0), jnp.logical_and(lane >= 96, place[0] == 31)
    )
    for m in range(10):
        product = conv_tiles(weights, 0, wide, 2 * m)
        for half in range(2):
            row = 2 * m + half
            value = leaky(add_y_taps(product[:, tiles(half)]) + bias[0])
            gone = outside
            if row < 2:
                gone = jnp.logical_or(outside, place[1] == 0)
            if row >= 18:
                gone = jnp.logical_or(outside, place[1] == 7)
            value = jnp.where(gone, 0.0, value)
            swapped = pltpu.roll(value, 64, 1).astype(BF16)
            if row < 12:
                left = slice(row * 128, row * 128 + 64)
                act[0:64, left] = value.astype(BF16)[:, 0:64]
                act[64:128, left] = pltpu.roll(value, 96, 1).astype(BF16)[:, 0:64]
                act[128:192, left] = swapped[:, 0:64]
            if row >= 8:
                right = slice((row - 8) * 128 + 64, (row - 8) * 128 + 128)
                act[0:64, right] = swapped[:, 64:128]
                act[64:128, right] = pltpu.roll(value, 32, 1).astype(BF16)[:, 64:128]
                act[128:192, right] = value.astype(BF16)[:, 64:128]

    front = lane % 64 < 32
    for m in range(5):
        product = conv_tiles(weights, 576, act, 2 * m)
        grads = []
        for half in range(2):
            row = 2 * m + half
            value = add_y_taps(product[:, tiles(half)]) + bias[1]
            cot = cotangent[row].astype(F32)
            grad = jnp.where(value > 0, cot, SLOPE * cot).astype(BF16)
            delta[row] = grad
            grads.append(grad.astype(F32))
            post[row] = leaky(value)
        to_prev = jnp.where(front, grads[0], pltpu.roll(grads[1], 32, 1))
        to_next = jnp.where(front, pltpu.roll(grads[0], 96, 1), grads[1])
        to_even[m] = jnp.where(upper, to_prev, to_next).astype(BF16)
        to_odd[m] = jnp.where(upper, to_next, to_prev).astype(BF16)

    for block in range(8):
        turn = lax.rem(block // 2 + 4 - place[4], 4)
        same = jnp.where(place[2] == block % 2, 0, 1)
        piece = [post[z + 1, 8 * block : 8 * block + 8] for z in range(8)]
        feats[turn, same] = jnp.concatenate(piece, axis=0).astype(BF16)


def kernel_grad(stacked, wide, start):
    products = [
        lax.dot_general(
            stacked[...],
            wide[:, tiles(start + dz, 8)],
            CONTRACT_LAST,
            preferred_element_type=F32,
        )
        for dz in range(3)
    ]
    return jnp.concatenate(products, axis=1)


def second_grad_kernel(delta, act, wide, out, total, narrow, stacked):
    low = lanes((192, 128)) < 64
    for k in range(8):
        value = delta[k + 1].astype(F32)
        stacked[:, tiles(k)] = stack_y(value)
        total[...] = value if k == 0 else total[...] + value
    out[...] = kernel_grad(stacked, act, 1)
    for k in range(10):
        left = pltpu.roll(wide[:, tiles(k + 2)].astype(F32), 96, 1)
        right = pltpu.roll(wide[:, tiles(k + 10)].astype(F32), 32, 1)
        narrow[:, tiles(k)] = jnp.where(low, left, right).astype(BF16)


def backward_kernel(
    place, delta, from_even, from_odd, weights, act, narrow, grad_two, total_two, keep, send, stacked, own, both
):
    lane = lanes((64, 128))
    upper = lax.rem(place[0], 2) == 1
    front = lane % 64 < 32
    for m in range(5):
        x, y = (from_even[m].astype(F32), from_odd[m].astype(F32))
        prev, after = (jnp.where(upper, x, y), jnp.where(upper, y, x))
        for half in range(2):
            row = 2 * m + half
            value = delta[row].astype(F32)
            left = pltpu.roll(prev, 96, 1) if half else prev
            right = after if half else pltpu.roll(after, 32, 1)
            minus = jnp.where(front, left, pltpu.roll(value, 32, 1))
            plus = jnp.where(front, pltpu.roll(value, 96, 1), right)
            stacked[0:64, tiles(row)] = minus.astype(BF16)
            stacked[64:128, tiles(row)] = delta[row]
            stacked[128:192, tiles(row)] = plus.astype(BF16)

    total = jnp.zeros((64, 128), F32)
    for m in range(4):
        product = conv_tiles(weights, 0, stacked, 2 * m)
        for half in range(2):
            back = add_y_taps(product[:, tiles(half)])
            positive = act[64:128, tiles(2 * m + 2 + half)].astype(F32) > 0
            value = jnp.where(positive, back, SLOPE * back).astype(BF16).astype(F32)
            own[:, tiles(2 * m + half)] = stack_y(value)
            total = total + value

    both[:, 0:576] = grad_two[...]
    both[:, 576:1152] = kernel_grad(own, narrow, 0)
    offsets = jnp.where(
        lane == 0,
        jnp.sum(total_two[...], axis=1, keepdims=True),
        jnp.sum(total, axis=1, keepdims=True),
    )
    def block(index):
        rows = [both[24 * index + 8 * (u // 9) : 24 * index + 8 * (u // 9) + 8, tiles(u % 9)] for u in range(27)]
        return jnp.concatenate(rows + [offsets[8 * index : 8 * index + 8]], axis=0)

    first = place[2] == 0
    for group in range(4):
        even, odd = (block(2 * group), block(2 * group + 1))
        turn = lax.rem(group + 4 - place[4], 4)
        keep[turn] = jnp.where(first, even, odd).astype(BF16)
        send[turn] = jnp.where(first, odd, even).astype(BF16)


def sum_of_four(parts):
    parts = [part.astype(F32) for part in parts]
    return (parts[0] + parts[2]) + (parts[1] + parts[3])


def finish_kernel(factor, first, second, third, fourth, kernel_two, kernel_one, offsets):
    total = sum_of_four([first[...], second[...], third[...], fourth[...]]) * factor
    units = [total[8 * u : 8 * u + 8] for u in range(28)]
    for dy in range(3):
        for column in range(9):
            value = units[dy * 9 + column]
            for half in range(2):
                layer, k = divmod(2 * column + half, 9)
                dz, dx = divmod(k, 3)
                target = kernel_one if layer else kernel_two
                target[dx * 9 + dy * 3 + dz] = value[:, 64 * half : 64 * half + 64]
    offsets[...] = units[27]


def features_kernel(place, *refs):
    pieces, other, out, turned = (refs[:4], refs[4:8], refs[8], refs[9])
    for k in range(4):
        group = lax.rem(place[4] + 4 - k, 4)
        group = jnp.where(place[3] == 1, 3 - group, group)
        for same in range(2):
            value = (other[k][1] if same else pieces[k][0]).astype(F32)
            core = place[2] if same == 0 else 1 - place[2]
            start = pl.multiple_of(128 * (2 * group + core), 128)
            turned[pl.ds(start, 64), :] = value
            turned[pl.ds(start + 64, 64), :] = pltpu.roll(value, 64, 1)
    for o in range(8):
        out[o] = turned[pl.ds(o, 128, stride=8), :].T[0:64].astype(BF16)


def call(kernel, out_shapes, scratch, *args, scalars=(), far=(), flops=0, limit=VMEM_LIMIT):
    vmem = pl.BlockSpec(memory_space=pltpu.VMEM)
    smem = pl.BlockSpec(memory_space=pltpu.SMEM)
    anywhere = pl.BlockSpec(memory_space=pltpu.HBM)
    outs = [jax.ShapeDtypeStruct(shape, dtype) for shape, dtype in out_shapes]
    size = sum(a.size * a.dtype.itemsize for a in args)
    size += sum(o.size * o.dtype.itemsize for o in outs)
    return pl.pallas_call(
        kernel,
        out_shape=outs,
        in_specs=[smem if k in scalars else anywhere if k in far else vmem for k in range(len(args))],
        out_specs=[vmem] * len(outs),
        scratch_shapes=[pltpu.VMEM(*x) if isinstance(x, tuple) else x for x in scratch],
        compiler_params=pltpu.CompilerParams(vmem_limit_bytes=limit),
        cost_estimate=pl.CostEstimate(flops=flops, bytes_accessed=size, transcendentals=0),
    )(*args)


def neighbours():
    both = []
    for start in range(2):
        pairs = []
        for here in range(start, 31, 2):
            there = here + 1
            turn = (here // 4) % 2 != (there // 4) % 2
            for l in range(4):
                pair = (here * 4 + l, there * 4 + (3 - l if turn else l))
                pairs += [pair, pair[::-1]]
        both.append(pairs)
    return both


def shards(volume, weight_one, bias_one, weight_two, bias_two, cotangent):
    factor = float(volume.shape[1] * 32 * volume.shape[2] * volume.shape[3]) ** (-0.5)
    h, l, c = (lax.axis_index(name) for name in ("h", "l", "c"))
    mirrored = h == 1
    block = 2 * jnp.where(mirrored, 3 - l, l) + c
    place = [lax.axis_index(SPACE), block, c, h, l]
    place = jnp.stack(place).astype(jnp.int32)
    even, odd = neighbours()
    near = SPACE + ("l",)
    swap = [(0, 1), (1, 0)]

    def spread(pieces, axis="l"):
        turns = [[(i, (i + k) % 4) for i in range(4)] for k in range(4)]
        return [pieces[0]] + [lax.ppermute(pieces[k], axis, turns[k]) for k in range(1, 4)]

    def cross(pieces):
        return [lax.ppermute(piece, "c", swap) for piece in pieces]

    (pieces,) = call(
        volume_kernel,
        [((4, 2, 88, 128), BF16)],
        [((8, 64, 128), BF16), ((1072, 128), F32), pltpu.SemaphoreType.DMA(())],
        place,
        volume.reshape(8, 64, 128),
        scalars=(0,),
        far=(1,),
    )
    pieces = spread([pieces[k] for k in range(4)])
    (field,) = call(
        unpack_kernel,
        [((11, 64, 128), BF16)],
        [],
        place,
        *pieces,
        *cross(pieces),
        scalars=(0,),
    )
    near_even = lax.ppermute(field, near, even)
    near_odd = lax.ppermute(field, near, odd)

    rest = call(
        rest_kernel,
        [((384, 128), BF16)] * 4,
        [
            ((8, 64, 128), BF16),
            ((1072, 128), F32),
            ((2, 27, 8, 64), BF16),
            pltpu.SMEM((2, 8), F32),
            pltpu.SemaphoreType.DMA((5,)),
        ],
        place,
        cotangent.reshape(8, 64, 128),
        jnp.transpose(weight_one, (2, 3, 4, 0, 1)).reshape(27, 8, 64),
        bias_one,
        jnp.transpose(weight_two, (2, 3, 4, 0, 1)).reshape(27, 8, 64),
        bias_two,
        scalars=(0,),
        far=(1, 2, 3, 4, 5),
        limit=FULL_LIMIT,
    )
    rest = spread(rest)
    weights, weights_back, bias, cots = call(
        weights_kernel,
        [((192, 1152), BF16), ((192, 576), BF16), ((2, 64, 128), F32), ((10, 64, 128), BF16)],
        [],
        place,
        *rest,
        *cross(rest),
        scalars=(0,),
    )

    act, wide, delta, feats, to_even, to_odd = call(
        forward_kernel,
        [
            ((192, 1536), BF16),
            ((192, 2816), BF16),
            ((10, 64, 128), BF16),
            ((4, 2, 64, 128), BF16),
            ((5, 64, 128), BF16),
            ((5, 64, 128), BF16),
        ],
        [((10, 64, 128), F32)],
        place,
        field,
        near_even,
        near_odd,
        cots,
        weights,
        bias,
        scalars=(0,),
        flops=2 * 192 * 576 * 128 * 30,
    )
    from_even = lax.ppermute(to_even, near, even)
    from_odd = lax.ppermute(to_odd, near, odd)
    grad_two, total_two, narrow = call(
        second_grad_kernel,
        [((192, 576), F32), ((64, 128), F32), ((192, 1280), BF16)],
        [((192, 1024), BF16)],
        delta,
        act,
        wide,
        flops=2 * 192 * 576 * 1024,
    )
    keep, send = call(
        backward_kernel,
        [((4, 224, 128), BF16), ((4, 224, 128), BF16)],
        [((192, 1280), BF16), ((192, 1024), BF16), ((192, 1152), F32)],
        place,
        delta,
        from_even,
        from_odd,
        weights_back,
        act,
        narrow,
        grad_two,
        total_two,
        scalars=(0,),
        flops=4 * 192 * 576 * 1024,
    )

    other = lax.ppermute(send, "c", swap)
    parts = [(keep[k].astype(F32) + other[k].astype(F32)).astype(BF16) for k in range(4)]
    part = sum_of_four(spread(parts)).astype(BF16)
    other = lax.ppermute(part, "h", swap)
    part = (part.astype(F32) + other.astype(F32)).astype(BF16)
    part = sum_of_four(spread([part] * 4, "y")).astype(BF16)
    parts = spread([part] * 4, "x")
    kernel_two, kernel_one, offsets = call(
        functools.partial(finish_kernel, factor),
        [((27, 8, 64), F32), ((27, 8, 64), F32), ((8, 128), F32)],
        [],
        *parts,
    )
    kernel_one, kernel_two = (
        jnp.transpose(k.reshape(3, 3, 3, 8, 64), (3, 4, 0, 1, 2)) for k in (kernel_one, kernel_two)
    )

    feats = spread([feats[k] for k in range(4)])
    (features,) = call(
        features_kernel,
        [((8, 64, 128), BF16)],
        [((1024, 128), F32)],
        place,
        *feats,
        *cross(feats),
        scalars=(0,),
    )
    return features.reshape(8, 2, 32, 128), kernel_one, offsets[:, 1], kernel_two, offsets[:, 0]


def solution(mesh):
    fine = Mesh(mesh.devices.reshape(4, 2, 4, 4, 2), ("x", "h", "y", "l", "c"))
    field = P(CHAN, SPACE, None, None)
    kernel = P(CHAN, None, None, None, None)
    in_specs = (field, kernel, P(CHAN), kernel, P(CHAN), field)
    out_specs = (field, kernel, P(CHAN), kernel, P(CHAN))
    return jax.shard_map(shards, mesh=fine, in_specs=in_specs, out_specs=out_specs, check_vma=False)
```

```python
import functools

import jax
import jax.numpy as jnp
from jax import lax
from jax.experimental import pallas as pl
from jax.experimental.pallas import tpu as pltpu
from jax.sharding import Mesh, PartitionSpec as P

SLOPE = 0.2
F32 = jnp.float32
BF16 = jnp.bfloat16
SPACE = ("x", "h", "y")
PLANE = ("x", "y")
CHAN = ("l", "c")
CONTRACT_LAST = (((1,), (1,)), ((), ()))
VMEM_LIMIT = 48 * 1024 * 1024
FULL_LIMIT = 63 * 1024 * 1024


def position():
    h, l, c = (lax.axis_index(name) for name in ("h", "l", "c"))
    space = (lax.axis_index("x") * 2 + h) * 4 + lax.axis_index("y")
    block = 2 * jnp.where(h == 1, 3 - l, l) + c
    return space, block, c, h, l


def leaky(value):
    return jnp.maximum(value, SLOPE * value)


def lanes(shape):
    return lax.broadcasted_iota(jnp.int32, shape, 1)


def tiles(index, count=1):
    return slice(index * 128, (index + count) * 128)


def along_y(array, step):
    y = lanes(array.shape) % 32
    edge = 0 if step == 1 else 31
    moved = pltpu.roll(array, step % array.shape[1], 1)
    return jnp.where(y == edge, 0.0, moved)


def add_y_taps(product):
    width = product.shape[1]
    split = product.reshape(8, 3, 8, width)
    below, middle, above = (split[:, k].reshape(64, width) for k in range(3))
    return middle + along_y(below, 1) + along_y(above, -1)


def stack_y(delta):
    parts = [along_y(delta, -1), delta, along_y(delta, 1)]
    parts = [part.reshape(8, 1, 8, part.shape[1]) for part in parts]
    return jnp.concatenate(parts, axis=1).reshape(192, delta.shape[1]).astype(BF16)


def conv_tiles(weights, column, stacked, start):
    return sum(
        jnp.dot(
            weights[:, column + dz * 192 : column + dz * 192 + 192],
            stacked[:, tiles(start + dz, 2)],
            preferred_element_type=F32,
        )
        for dz in range(3)
    )


def turn_field(place, held, turned):
    turned[0:24] = jnp.zeros((24, 128), F32)
    turned[1048:1072] = jnp.zeros((24, 128), F32)
    for ch in range(8):
        value = held[ch].astype(F32)
        turned[pl.ds(24 + ch, 128, stride=8), :] = jnp.concatenate([value, value], axis=0).T


def target_of(place, block):
    chip = jnp.where(place[3] == 1, 3 - block // 2, block // 2)
    return lax.rem(chip + 4 - place[4], 4), jnp.where(place[2] == block % 2, 0, 1)


def volume_kernel(volume, out, held, turned, arrived):
    place = position()
    copy = pltpu.make_async_copy(volume, held, arrived)
    copy.start()
    low = lanes((88, 128)) < 64
    copy.wait()
    turn_field(place, held, turned)
    for block in range(8):
        turn, same = target_of(place, block)
        rows = turned[block * 128 : block * 128 + 176].reshape(11, 2, 8, 128)
        even, odd = (rows[:, k].reshape(88, 128) for k in range(2))
        out[turn, same] = jnp.where(low, even, odd).astype(BF16)


def rest_kernel(
    cotangent,
    weight_one,
    bias_one,
    weight_two,
    bias_two,
    first,
    second,
    third,
    fourth,
    held,
    turned,
    kernels,
    biases,
    arrived,
):
    place = position()
    copies = [
        pltpu.make_async_copy(ref, to, arrived.at[k])
        for k, (ref, to) in enumerate(
            (
                (cotangent, held),
                (weight_one, kernels.at[0]),
                (weight_two, kernels.at[1]),
                (bias_one, biases.at[0]),
                (bias_two, biases.at[1]),
            )
        )
    ]
    for copy in copies:
        copy.start()
    for copy in copies:
        copy.wait()

    row = lax.broadcasted_iota(jnp.int32, (8, 128), 0)
    lane = lanes((8, 128))
    rows = []
    for t in range(9):
        for dy in range(3):
            halves = []
            for half in range(2):
                layer, k = divmod(2 * t + half, 9)
                dz, dx = divmod(k, 3)
                halves.append(kernels[layer, dx * 9 + dy * 3 + dz].astype(F32))
            rows.append(jnp.concatenate(halves, axis=1))
    packed = jnp.zeros((8, 128), F32)
    for layer in range(2):
        value = sum(jnp.where(row == o, biases[layer, o], 0.0) for o in range(8))
        for part in range(3):
            rounded = value.astype(BF16).astype(F32)
            packed = jnp.where(lane == 3 * layer + part, rounded, packed)
            value = value - rounded
    rows.append(packed)
    turn_field(place, held, turned)
    low = lanes((80, 128)) < 64
    for k, out in enumerate((first, second, third, fourth)):
        chip = lax.rem(place[4] + k, 4)
        chip = jnp.where(place[3] == 1, 3 - chip, chip)
        pieces = []
        for same in range(2):
            block = 2 * chip + (1 - place[2] if same else place[2])
            start = pl.multiple_of(block * 128, 128)
            pieces.append(jnp.where(low, turned[pl.ds(start + 16, 80)], turned[pl.ds(start + 80, 80)]))
        out[...] = jnp.concatenate(pieces + rows, axis=0).astype(BF16)


def channel_order(place, ours, theirs):
    first = place[2] == 0
    pieces = [None] * 8
    pairs = [(jnp.where(first, a, b), jnp.where(first, b, a)) for a, b in zip(ours, theirs)]
    for chip in range(4):
        turn = lax.rem(place[4] + 4 - chip, 4)
        for core in range(2):
            value = pairs[3][core]
            for k in range(3):
                value = jnp.where(turn == k, pairs[k][core], value)
            pieces[2 * chip + core] = value
    return pieces


def unpack_kernel(*refs):
    place = position()
    ours, theirs, field = (refs[:4], refs[4:8], refs[8])
    ours = [ref[0].astype(F32) for ref in ours]
    theirs = [ref[1].astype(F32) for ref in theirs]
    pieces = channel_order(place, ours, theirs)
    for j in range(11):
        both = jnp.concatenate([piece[8 * j : 8 * j + 8] for piece in pieces], axis=0)
        field[j] = both.astype(BF16)


def weights_kernel(*refs):
    place = position()
    ours, theirs = (refs[:4], refs[4:8])
    out, back, bias, cots = refs[8:]
    pieces = channel_order(
        place, [ref[0:80].astype(F32) for ref in ours], [ref[80:160].astype(F32) for ref in theirs]
    )
    for j in range(10):
        both = jnp.concatenate([piece[8 * j : 8 * j + 8] for piece in pieces], axis=0)
        cots[j] = both.astype(BF16)

    first = place[2] == 0
    for k in range(4):
        group = lax.rem(place[4] + 4 - k, 4)
        mine, other = (ref[160:384].astype(F32) for ref in (ours[k], theirs[k]))
        pair = (jnp.where(first, mine, other), jnp.where(first, other, mine))
        rows = pl.ds(pl.multiple_of(48 * group, 16), 48)
        for t in range(9):
            block = jnp.concatenate([x[24 * t : 24 * t + 24] for x in pair], axis=0)
            out[rows, tiles(t)] = block.astype(BF16)
        extra = jnp.concatenate([x[216:224] for x in pair], axis=0)
        rows = pl.ds(pl.multiple_of(16 * group, 16), 16)
        for layer in range(2):
            parts = [extra[:, 3 * layer + k : 3 * layer + k + 1] for k in range(3)]
            bias[layer, rows] = jnp.broadcast_to(parts[0] + parts[1] + parts[2], (16, 128))
    kernel = out[:, 576:1152].astype(F32).reshape(8, 3, 8, 576)
    turned = [kernel[:, 2 - e].reshape(64, 576).T for e in range(3)]
    for column in range(9):
        block = [part[64 * (8 - column) : 64 * (8 - column) + 64].reshape(8, 1, 8, 64) for part in turned]
        block = jnp.concatenate(block, axis=1).reshape(192, 64)
        back[:, 64 * column : 64 * column + 64] = block.astype(BF16)


def forward_kernel(
    own, even, odd, cotangent, weights, bias, act, wide, delta, feats, to_even, to_odd, post
):
    place = position()
    upper = lax.rem(place[0], 2) == 1
    lane = lanes((64, 128))
    low = lane < 64

    for j in range(11):
        o, x, y = (ref[j].astype(F32) for ref in (own, even, odd))
        p, n = (jnp.where(upper, x, y), jnp.where(upper, y, x))
        turned = pltpu.roll(o, 64, 1)
        for half in range(2):
            if half == 0:
                minus = jnp.where(low, p, turned)
                plus = jnp.where(low, o, pltpu.roll(n, 64, 1))
            else:
                minus = jnp.where(low, pltpu.roll(p, 64, 1), o)
                plus = jnp.where(low, turned, n)
            zero = jnp.where(lane < 32, pltpu.roll(minus, 96, 1), pltpu.roll(plus, 32, 1))
            wide[0:64, tiles(2 * j + half)] = minus.astype(BF16)
            wide[64:128, tiles(2 * j + half)] = zero.astype(BF16)
            wide[128:192, tiles(2 * j + half)] = plus.astype(BF16)

    outside = jnp.logical_or(
        jnp.logical_and(lane < 32, place[0] == 0), jnp.logical_and(lane >= 96, place[0] == 31)
    )
    for m in range(10):
        product = conv_tiles(weights, 0, wide, 2 * m)
        for half in range(2):
            row = 2 * m + half
            value = leaky(add_y_taps(product[:, tiles(half)]) + bias[0])
            gone = outside
            if row < 2:
                gone = jnp.logical_or(outside, place[1] == 0)
            if row >= 18:
                gone = jnp.logical_or(outside, place[1] == 7)
            value = jnp.where(gone, 0.0, value)
            swapped = pltpu.roll(value, 64, 1).astype(BF16)
            if row < 12:
                left = slice(row * 128, row * 128 + 64)
                act[0:64, left] = value.astype(BF16)[:, 0:64]
                act[64:128, left] = pltpu.roll(value, 96, 1).astype(BF16)[:, 0:64]
                act[128:192, left] = swapped[:, 0:64]
            if row >= 8:
                right = slice((row - 8) * 128 + 64, (row - 8) * 128 + 128)
                act[0:64, right] = swapped[:, 64:128]
                act[64:128, right] = pltpu.roll(value, 32, 1).astype(BF16)[:, 64:128]
                act[128:192, right] = value.astype(BF16)[:, 64:128]

    front = lane % 64 < 32
    for m in range(5):
        product = conv_tiles(weights, 576, act, 2 * m)
        grads = []
        for half in range(2):
            row = 2 * m + half
            value = add_y_taps(product[:, tiles(half)]) + bias[1]
            cot = cotangent[row].astype(F32)
            grad = jnp.where(value > 0, cot, SLOPE * cot).astype(BF16)
            delta[row] = grad
            grads.append(grad.astype(F32))
            post[row] = leaky(value)
        to_prev = jnp.where(front, grads[0], pltpu.roll(grads[1], 32, 1))
        to_next = jnp.where(front, pltpu.roll(grads[0], 96, 1), grads[1])
        to_even[m] = jnp.where(upper, to_prev, to_next).astype(BF16)
        to_odd[m] = jnp.where(upper, to_next, to_prev).astype(BF16)

    for block in range(8):
        turn = lax.rem(block // 2 + 4 - place[4], 4)
        same = jnp.where(place[2] == block % 2, 0, 1)
        piece = [post[z + 1, 8 * block : 8 * block + 8] for z in range(8)]
        feats[turn, same] = jnp.concatenate(piece, axis=0).astype(BF16)


def kernel_grad(stacked, wide, start):
    products = [
        lax.dot_general(
            stacked[...],
            wide[:, tiles(start + dz, 8)],
            CONTRACT_LAST,
            preferred_element_type=F32,
        )
        for dz in range(3)
    ]
    return jnp.concatenate(products, axis=1)


def second_grad_kernel(delta, act, wide, out, total, narrow, stacked):
    low = lanes((192, 128)) < 64
    for k in range(8):
        value = delta[k + 1].astype(F32)
        stacked[:, tiles(k)] = stack_y(value)
        total[...] = value if k == 0 else total[...] + value
    out[...] = kernel_grad(stacked, act, 1)
    for k in range(10):
        left = pltpu.roll(wide[:, tiles(k + 2)].astype(F32), 96, 1)
        right = pltpu.roll(wide[:, tiles(k + 10)].astype(F32), 32, 1)
        narrow[:, tiles(k)] = jnp.where(low, left, right).astype(BF16)


def backward_kernel(
    delta, from_even, from_odd, weights, act, narrow, grad_two, total_two, keep, send, stacked, own, both
):
    place = position()
    lane = lanes((64, 128))
    upper = lax.rem(place[0], 2) == 1
    front = lane % 64 < 32
    for m in range(5):
        x, y = (from_even[m].astype(F32), from_odd[m].astype(F32))
        prev, after = (jnp.where(upper, x, y), jnp.where(upper, y, x))
        for half in range(2):
            row = 2 * m + half
            value = delta[row].astype(F32)
            left = pltpu.roll(prev, 96, 1) if half else prev
            right = after if half else pltpu.roll(after, 32, 1)
            minus = jnp.where(front, left, pltpu.roll(value, 32, 1))
            plus = jnp.where(front, pltpu.roll(value, 96, 1), right)
            stacked[0:64, tiles(row)] = minus.astype(BF16)
            stacked[64:128, tiles(row)] = delta[row]
            stacked[128:192, tiles(row)] = plus.astype(BF16)

    total = jnp.zeros((64, 128), F32)
    for m in range(4):
        product = conv_tiles(weights, 0, stacked, 2 * m)
        for half in range(2):
            back = add_y_taps(product[:, tiles(half)])
            positive = act[64:128, tiles(2 * m + 2 + half)].astype(F32) > 0
            value = jnp.where(positive, back, SLOPE * back).astype(BF16).astype(F32)
            own[:, tiles(2 * m + half)] = stack_y(value)
            total = total + value

    both[:, 0:576] = grad_two[...]
    both[:, 576:1152] = kernel_grad(own, narrow, 0)
    row = lax.broadcasted_iota(jnp.int32, (8, 64), 0)
    offsets = jnp.where(
        row == 0, jnp.sum(total_two[...].T, axis=0, keepdims=True), jnp.sum(total.T, axis=0, keepdims=True)
    )
    def block(index):
        rows = [both[24 * index + 8 * (u // 9) : 24 * index + 8 * (u // 9) + 8, tiles(u % 9)] for u in range(27)]
        last = jnp.concatenate([offsets[:, 8 * index : 8 * index + 8], jnp.zeros((8, 120), F32)], axis=1)
        return jnp.concatenate(rows + [last], axis=0)

    first = place[2] == 0
    for group in range(4):
        even, odd = (block(2 * group), block(2 * group + 1))
        turn = lax.rem(group + 4 - place[4], 4)
        keep[turn] = jnp.where(first, even, odd).astype(BF16)
        send[turn] = jnp.where(first, odd, even).astype(BF16)


def sum_of_four(parts):
    parts = [part.astype(F32) for part in parts]
    return (parts[0] + parts[2]) + (parts[1] + parts[3])


def finish_kernel(factor, first, second, third, fourth, kernel_two, kernel_one, two, one):
    total = sum_of_four([first[...], second[...], third[...], fourth[...]]) * factor
    units = [total[8 * u : 8 * u + 8] for u in range(28)]
    for dy in range(3):
        for column in range(9):
            value = units[dy * 9 + column]
            for half in range(2):
                layer, k = divmod(2 * column + half, 9)
                dz, dx = divmod(k, 3)
                target = kernel_one if layer else kernel_two
                target[dx * 9 + dy * 3 + dz] = value[:, 64 * half : 64 * half + 64]
    two[...] = units[27][0, 0:8]
    one[...] = units[27][1, 0:8]


def features_kernel(*refs):
    place = position()
    pieces, other, out, turned = (refs[:4], refs[4:8], refs[8], refs[9])
    for k in range(4):
        group = lax.rem(place[4] + 4 - k, 4)
        group = jnp.where(place[3] == 1, 3 - group, group)
        for same in range(2):
            value = (other[k][1] if same else pieces[k][0]).astype(F32)
            core = place[2] if same == 0 else 1 - place[2]
            start = pl.multiple_of(128 * (2 * group + core), 128)
            turned[pl.ds(start, 64), :] = value
            turned[pl.ds(start + 64, 64), :] = pltpu.roll(value, 64, 1)
    for o in range(8):
        out[o] = turned[pl.ds(o, 128, stride=8), :].T[0:64].astype(BF16)


def call(kernel, out_shapes, scratch, *args, scalars=(), far=(), flops=0, limit=VMEM_LIMIT):
    vmem = pl.BlockSpec(memory_space=pltpu.VMEM)
    smem = pl.BlockSpec(memory_space=pltpu.SMEM)
    anywhere = pl.BlockSpec(memory_space=pltpu.HBM)
    outs = [jax.ShapeDtypeStruct(shape, dtype) for shape, dtype in out_shapes]
    size = sum(a.size * a.dtype.itemsize for a in args)
    size += sum(o.size * o.dtype.itemsize for o in outs)
    return pl.pallas_call(
        kernel,
        out_shape=outs,
        in_specs=[smem if k in scalars else anywhere if k in far else vmem for k in range(len(args))],
        out_specs=[vmem] * len(outs),
        scratch_shapes=[pltpu.VMEM(*x) if isinstance(x, tuple) else x for x in scratch],
        compiler_params=pltpu.CompilerParams(vmem_limit_bytes=limit),
        cost_estimate=pl.CostEstimate(flops=flops, bytes_accessed=size, transcendentals=0),
    )(*args)


def neighbours():
    both = []
    for start in range(2):
        pairs = []
        for here in range(start, 31, 2):
            there = here + 1
            turn = (here // 4) % 2 != (there // 4) % 2
            for l in range(4):
                pair = (here * 4 + l, there * 4 + (3 - l if turn else l))
                pairs += [pair, pair[::-1]]
        both.append(pairs)
    return both


def shards(volume, weight_one, bias_one, weight_two, bias_two, cotangent):
    factor = float(volume.shape[1] * 32 * volume.shape[2] * volume.shape[3]) ** (-0.5)
    c = lax.axis_index("c")
    even, odd = neighbours()
    near = SPACE + ("l",)
    swap = [(0, 1), (1, 0)]

    def spread(pieces, axis="l"):
        turns = [[(i, (i + k) % 4) for i in range(4)] for k in range(4)]
        return [pieces[0]] + [lax.ppermute(pieces[k], axis, turns[k]) for k in range(1, 4)]

    def cross(pieces):
        return [lax.ppermute(piece, "c", swap) for piece in pieces]

    (pieces,) = call(
        volume_kernel,
        [((4, 2, 88, 128), BF16)],
        [((8, 64, 128), BF16), ((1072, 128), F32), pltpu.SemaphoreType.DMA(())],
        volume.reshape(8, 64, 128),
        far=(0,),
    )
    pieces = spread([pieces[k] for k in range(4)])
    (field,) = call(
        unpack_kernel,
        [((11, 64, 128), BF16)],
        [],
        *pieces,
        *cross(pieces),
    )
    near_even = lax.ppermute(field, near, even)
    near_odd = lax.ppermute(field, near, odd)

    rest = call(
        rest_kernel,
        [((384, 128), BF16)] * 4,
        [
            ((8, 64, 128), BF16),
            ((1072, 128), F32),
            ((2, 27, 8, 64), BF16),
            pltpu.SMEM((2, 8), F32),
            pltpu.SemaphoreType.DMA((5,)),
        ],
        cotangent.reshape(8, 64, 128),
        jnp.transpose(weight_one, (2, 3, 4, 0, 1)).reshape(27, 8, 64),
        bias_one,
        jnp.transpose(weight_two, (2, 3, 4, 0, 1)).reshape(27, 8, 64),
        bias_two,
        far=(0, 1, 2, 3, 4),
        limit=FULL_LIMIT,
    )
    rest = spread(rest)
    weights, weights_back, bias, cots = call(
        weights_kernel,
        [((192, 1152), BF16), ((192, 576), BF16), ((2, 64, 128), F32), ((10, 64, 128), BF16)],
        [],
        *rest,
        *cross(rest),
    )

    act, wide, delta, feats, to_even, to_odd = call(
        forward_kernel,
        [
            ((192, 1536), BF16),
            ((192, 2816), BF16),
            ((10, 64, 128), BF16),
            ((4, 2, 64, 128), BF16),
            ((5, 64, 128), BF16),
            ((5, 64, 128), BF16),
        ],
        [((10, 64, 128), F32)],
        field,
        near_even,
        near_odd,
        cots,
        weights,
        bias,
        flops=2 * 192 * 576 * 128 * 30,
    )
    from_even = lax.ppermute(to_even, near, even)
    from_odd = lax.ppermute(to_odd, near, odd)
    grad_two, total_two, narrow = call(
        second_grad_kernel,
        [((192, 576), F32), ((64, 128), F32), ((192, 1280), BF16)],
        [((192, 1024), BF16)],
        delta,
        act,
        wide,
        flops=2 * 192 * 576 * 1024,
    )
    feats = spread([feats[k] for k in range(4)])
    keep, send = call(
        backward_kernel,
        [((4, 224, 128), BF16), ((4, 224, 128), BF16)],
        [((192, 1280), BF16), ((192, 1024), BF16), ((192, 1152), F32)],
        delta,
        from_even,
        from_odd,
        weights_back,
        act,
        narrow,
        grad_two,
        total_two,
        flops=4 * 192 * 576 * 1024,
    )

    send, feats = lax.optimization_barrier((send, feats))
    other = lax.ppermute(send, "c", swap)
    parts = [(keep[k].astype(F32) + other[k].astype(F32)).astype(BF16) for k in range(4)]
    feats = feats + cross(feats)
    parts = spread(parts)
    parts, feats = lax.optimization_barrier((parts, feats))
    part = sum_of_four(parts).astype(BF16)
    other = lax.ppermute(part, "h", swap)
    part = (part.astype(F32) + other.astype(F32)).astype(BF16)
    part = sum_of_four(spread([part] * 4, "y")).astype(BF16)
    parts = spread([part] * 4, "x")
    kernel_two, kernel_one, offset_two, offset_one = call(
        functools.partial(finish_kernel, factor),
        [((27, 8, 64), F32), ((27, 8, 64), F32), ((8,), F32), ((8,), F32)],
        [],
        *parts,
    )
    kernel_one, kernel_two = (
        jnp.transpose(k.reshape(3, 3, 3, 8, 64), (3, 4, 0, 1, 2)) for k in (kernel_one, kernel_two)
    )

    (features,) = call(
        features_kernel,
        [((8, 64, 128), BF16)],
        [((1024, 128), F32)],
        *feats,
    )
    return features.reshape(8, 2, 32, 128), kernel_one, offset_one, kernel_two, offset_two


def solution(mesh):
    fine = Mesh(mesh.devices.reshape(4, 2, 4, 4, 2), ("x", "h", "y", "l", "c"))
    field = P(CHAN, SPACE, None, None)
    kernel = P(CHAN, None, None, None, None)
    in_specs = (field, kernel, P(CHAN), kernel, P(CHAN), field)
    out_specs = (field, kernel, P(CHAN), kernel, P(CHAN))
    return jax.shard_map(shards, mesh=fine, in_specs=in_specs, out_specs=out_specs, check_vma=False)
```

```python
import functools

import jax
import jax.numpy as jnp
from jax import lax
from jax.experimental import pallas as pl
from jax.experimental.pallas import tpu as pltpu
from jax.sharding import Mesh, PartitionSpec as P

SLOPE = 0.2
F32 = jnp.float32
BF16 = jnp.bfloat16
SPACE = ("x", "h", "y")
PLANE = ("x", "y")
CHAN = ("l", "c")
CONTRACT_LAST = (((1,), (1,)), ((), ()))
VMEM_LIMIT = 48 * 1024 * 1024
FULL_LIMIT = 63 * 1024 * 1024


def position():
    h, l, c = (lax.axis_index(name) for name in ("h", "l", "c"))
    space = (lax.axis_index("x") * 2 + h) * 4 + lax.axis_index("y")
    block = 2 * jnp.where(h == 1, 3 - l, l) + c
    return space, block, c, h, l


def leaky(value):
    return jnp.maximum(value, SLOPE * value)


def lanes(shape):
    return lax.broadcasted_iota(jnp.int32, shape, 1)


def tiles(index, count=1):
    return slice(index * 128, (index + count) * 128)


def along_y(array, step):
    y = lanes(array.shape) % 32
    edge = 0 if step == 1 else 31
    moved = pltpu.roll(array, step % array.shape[1], 1)
    return jnp.where(y == edge, 0.0, moved)


def add_y_taps(product):
    width = product.shape[1]
    split = product.reshape(8, 3, 8, width)
    below, middle, above = (split[:, k].reshape(64, width) for k in range(3))
    return middle + along_y(below, 1) + along_y(above, -1)


def stack_y(delta):
    parts = [along_y(delta, -1), delta, along_y(delta, 1)]
    parts = [part.reshape(8, 1, 8, part.shape[1]) for part in parts]
    return jnp.concatenate(parts, axis=1).reshape(192, delta.shape[1]).astype(BF16)


def conv_tiles(weights, column, stacked, start):
    return sum(
        jnp.dot(
            weights[:, column + dz * 192 : column + dz * 192 + 192],
            stacked[:, tiles(start + dz, 2)],
            preferred_element_type=F32,
        )
        for dz in range(3)
    )


def turn_field(place, held, turned):
    turned[0:24] = jnp.zeros((24, 128), F32)
    turned[1048:1072] = jnp.zeros((24, 128), F32)
    for ch in range(8):
        value = held[ch].astype(F32)
        turned[pl.ds(24 + ch, 128, stride=8), :] = jnp.concatenate([value, value], axis=0).T


def target_of(place, block):
    chip = jnp.where(place[3] == 1, 3 - block // 2, block // 2)
    return lax.rem(chip + 4 - place[4], 4), jnp.where(place[2] == block % 2, 0, 1)


def volume_kernel(volume, out, held, turned, arrived):
    place = position()
    copy = pltpu.make_async_copy(volume, held, arrived)
    copy.start()
    low = lanes((88, 128)) < 64
    copy.wait()
    turn_field(place, held, turned)
    for block in range(8):
        turn, same = target_of(place, block)
        rows = turned[block * 128 : block * 128 + 176].reshape(11, 2, 8, 128)
        even, odd = (rows[:, k].reshape(88, 128) for k in range(2))
        out[turn, same] = jnp.where(low, even, odd).astype(BF16)


def rest_kernel(
    cotangent,
    weight_one,
    bias_one,
    weight_two,
    bias_two,
    first,
    second,
    third,
    fourth,
    held,
    turned,
    kernels,
    biases,
    arrived,
):
    place = position()
    copies = [
        pltpu.make_async_copy(ref, to, arrived.at[k])
        for k, (ref, to) in enumerate(
            (
                (cotangent, held),
                (weight_one, kernels.at[0]),
                (weight_two, kernels.at[1]),
                (bias_one, biases.at[0]),
                (bias_two, biases.at[1]),
            )
        )
    ]
    for copy in copies:
        copy.start()
    for copy in copies:
        copy.wait()

    row = lax.broadcasted_iota(jnp.int32, (8, 128), 0)
    lane = lanes((8, 128))
    rows = []
    for t in range(9):
        for dy in range(3):
            halves = []
            for half in range(2):
                layer, k = divmod(2 * t + half, 9)
                dz, dx = divmod(k, 3)
                halves.append(kernels[layer, dx * 9 + dy * 3 + dz].astype(F32))
            rows.append(jnp.concatenate(halves, axis=1))
    packed = jnp.zeros((8, 128), F32)
    for layer in range(2):
        value = sum(jnp.where(row == o, biases[layer, o], 0.0) for o in range(8))
        for part in range(3):
            rounded = value.astype(BF16).astype(F32)
            packed = jnp.where(lane == 3 * layer + part, rounded, packed)
            value = value - rounded
    rows.append(packed)
    turn_field(place, held, turned)
    low = lanes((80, 128)) < 64
    for k, out in enumerate((first, second, third, fourth)):
        chip = lax.rem(place[4] + k, 4)
        chip = jnp.where(place[3] == 1, 3 - chip, chip)
        pieces = []
        for same in range(2):
            block = 2 * chip + (1 - place[2] if same else place[2])
            start = pl.multiple_of(block * 128, 128)
            pieces.append(jnp.where(low, turned[pl.ds(start + 16, 80)], turned[pl.ds(start + 80, 80)]))
        out[...] = jnp.concatenate(pieces + rows, axis=0).astype(BF16)


def channel_order(place, ours, theirs):
    first = place[2] == 0
    pieces = [None] * 8
    pairs = [(jnp.where(first, a, b), jnp.where(first, b, a)) for a, b in zip(ours, theirs)]
    for chip in range(4):
        turn = lax.rem(place[4] + 4 - chip, 4)
        for core in range(2):
            value = pairs[3][core]
            for k in range(3):
                value = jnp.where(turn == k, pairs[k][core], value)
            pieces[2 * chip + core] = value
    return pieces


def unpack_kernel(*refs):
    place = position()
    ours, theirs, field = (refs[:4], refs[4:8], refs[8])
    ours = [ref[0].astype(F32) for ref in ours]
    theirs = [ref[1].astype(F32) for ref in theirs]
    pieces = channel_order(place, ours, theirs)
    for j in range(11):
        both = jnp.concatenate([piece[8 * j : 8 * j + 8] for piece in pieces], axis=0)
        field[j] = both.astype(BF16)


def weights_kernel(*refs):
    place = position()
    ours, theirs = (refs[:4], refs[4:8])
    out, back, bias, cots = refs[8:]
    pieces = channel_order(
        place, [ref[0:80].astype(F32) for ref in ours], [ref[80:160].astype(F32) for ref in theirs]
    )
    for j in range(10):
        both = jnp.concatenate([piece[8 * j : 8 * j + 8] for piece in pieces], axis=0)
        cots[j] = both.astype(BF16)

    first = place[2] == 0
    for k in range(4):
        group = lax.rem(place[4] + 4 - k, 4)
        mine, other = (ref[160:384].astype(F32) for ref in (ours[k], theirs[k]))
        pair = (jnp.where(first, mine, other), jnp.where(first, other, mine))
        rows = pl.ds(pl.multiple_of(48 * group, 16), 48)
        for t in range(9):
            block = jnp.concatenate([x[24 * t : 24 * t + 24] for x in pair], axis=0)
            out[rows, tiles(t)] = block.astype(BF16)
        extra = jnp.concatenate([x[216:224] for x in pair], axis=0)
        rows = pl.ds(pl.multiple_of(16 * group, 16), 16)
        for layer in range(2):
            parts = [extra[:, 3 * layer + k : 3 * layer + k + 1] for k in range(3)]
            bias[layer, rows] = jnp.broadcast_to(parts[0] + parts[1] + parts[2], (16, 128))
    kernel = out[:, 576:1152].astype(F32).reshape(8, 3, 8, 576)
    turned = [kernel[:, 2 - e].reshape(64, 576).T for e in range(3)]
    for column in range(9):
        block = [part[64 * (8 - column) : 64 * (8 - column) + 64].reshape(8, 1, 8, 64) for part in turned]
        block = jnp.concatenate(block, axis=1).reshape(192, 64)
        back[:, 64 * column : 64 * column + 64] = block.astype(BF16)


def forward_kernel(
    own, even, odd, cotangent, weights, bias, act, wide, delta, feats, to_even, to_odd, post
):
    place = position()
    upper = lax.rem(place[0], 2) == 1
    lane = lanes((64, 128))
    low = lane < 64

    for j in range(11):
        o, x, y = (ref[j].astype(F32) for ref in (own, even, odd))
        p, n = (jnp.where(upper, x, y), jnp.where(upper, y, x))
        turned = pltpu.roll(o, 64, 1)
        for half in range(2):
            if half == 0:
                minus = jnp.where(low, p, turned)
                plus = jnp.where(low, o, pltpu.roll(n, 64, 1))
            else:
                minus = jnp.where(low, pltpu.roll(p, 64, 1), o)
                plus = jnp.where(low, turned, n)
            zero = jnp.where(lane < 32, pltpu.roll(minus, 96, 1), pltpu.roll(plus, 32, 1))
            wide[0:64, tiles(2 * j + half)] = minus.astype(BF16)
            wide[64:128, tiles(2 * j + half)] = zero.astype(BF16)
            wide[128:192, tiles(2 * j + half)] = plus.astype(BF16)

    outside = jnp.logical_or(
        jnp.logical_and(lane < 32, place[0] == 0), jnp.logical_and(lane >= 96, place[0] == 31)
    )
    for m in range(10):
        product = conv_tiles(weights, 0, wide, 2 * m)
        for half in range(2):
            row = 2 * m + half
            value = leaky(add_y_taps(product[:, tiles(half)]) + bias[0])
            gone = outside
            if row < 2:
                gone = jnp.logical_or(outside, place[1] == 0)
            if row >= 18:
                gone = jnp.logical_or(outside, place[1] == 7)
            value = jnp.where(gone, 0.0, value)
            swapped = pltpu.roll(value, 64, 1).astype(BF16)
            if row < 12:
                left = slice(row * 128, row * 128 + 64)
                act[0:64, left] = value.astype(BF16)[:, 0:64]
                act[64:128, left] = pltpu.roll(value, 96, 1).astype(BF16)[:, 0:64]
                act[128:192, left] = swapped[:, 0:64]
            if row >= 8:
                right = slice((row - 8) * 128 + 64, (row - 8) * 128 + 128)
                act[0:64, right] = swapped[:, 64:128]
                act[64:128, right] = pltpu.roll(value, 32, 1).astype(BF16)[:, 64:128]
                act[128:192, right] = value.astype(BF16)[:, 64:128]

    front = lane % 64 < 32
    for m in range(5):
        product = conv_tiles(weights, 576, act, 2 * m)
        grads = []
        for half in range(2):
            row = 2 * m + half
            value = add_y_taps(product[:, tiles(half)]) + bias[1]
            cot = cotangent[row].astype(F32)
            grad = jnp.where(value > 0, cot, SLOPE * cot).astype(BF16)
            delta[row] = grad
            grads.append(grad.astype(F32))
            post[row] = leaky(value)
        to_prev = jnp.where(front, grads[0], pltpu.roll(grads[1], 32, 1))
        to_next = jnp.where(front, pltpu.roll(grads[0], 96, 1), grads[1])
        to_even[m] = jnp.where(upper, to_prev, to_next).astype(BF16)
        to_odd[m] = jnp.where(upper, to_next, to_prev).astype(BF16)

    for block in range(8):
        turn = lax.rem(block // 2 + 4 - place[4], 4)
        same = jnp.where(place[2] == block % 2, 0, 1)
        piece = [post[z + 1, 8 * block : 8 * block + 8] for z in range(8)]
        feats[turn, same] = jnp.concatenate(piece, axis=0).astype(BF16)


def kernel_grad(stacked, wide, start):
    products = [
        lax.dot_general(
            stacked[...],
            wide[:, tiles(start + dz, 8)],
            CONTRACT_LAST,
            preferred_element_type=F32,
        )
        for dz in range(3)
    ]
    return jnp.concatenate(products, axis=1)


def second_grad_kernel(delta, act, wide, out, total, narrow, stacked):
    low = lanes((192, 128)) < 64
    for k in range(8):
        value = delta[k + 1].astype(F32)
        stacked[:, tiles(k)] = stack_y(value)
        total[...] = value if k == 0 else total[...] + value
    out[...] = kernel_grad(stacked, act, 1)
    for k in range(10):
        left = pltpu.roll(wide[:, tiles(k + 2)].astype(F32), 96, 1)
        right = pltpu.roll(wide[:, tiles(k + 10)].astype(F32), 32, 1)
        narrow[:, tiles(k)] = jnp.where(low, left, right).astype(BF16)


def backward_kernel(
    delta, from_even, from_odd, weights, act, narrow, grad_two, total_two, keep, send, stacked, own, both
):
    place = position()
    lane = lanes((64, 128))
    upper = lax.rem(place[0], 2) == 1
    front = lane % 64 < 32
    for m in range(5):
        x, y = (from_even[m].astype(F32), from_odd[m].astype(F32))
        prev, after = (jnp.where(upper, x, y), jnp.where(upper, y, x))
        for half in range(2):
            row = 2 * m + half
            value = delta[row].astype(F32)
            left = pltpu.roll(prev, 96, 1) if half else prev
            right = after if half else pltpu.roll(after, 32, 1)
            minus = jnp.where(front, left, pltpu.roll(value, 32, 1))
            plus = jnp.where(front, pltpu.roll(value, 96, 1), right)
            stacked[0:64, tiles(row)] = minus.astype(BF16)
            stacked[64:128, tiles(row)] = delta[row]
            stacked[128:192, tiles(row)] = plus.astype(BF16)

    total = jnp.zeros((64, 128), F32)
    for m in range(4):
        product = conv_tiles(weights, 0, stacked, 2 * m)
        for half in range(2):
            back = add_y_taps(product[:, tiles(half)])
            positive = act[64:128, tiles(2 * m + 2 + half)].astype(F32) > 0
            value = jnp.where(positive, back, SLOPE * back).astype(BF16).astype(F32)
            own[:, tiles(2 * m + half)] = stack_y(value)
            total = total + value

    both[:, 0:576] = grad_two[...]
    both[:, 576:1152] = kernel_grad(own, narrow, 0)
    row = lax.broadcasted_iota(jnp.int32, (8, 64), 0)
    offsets = jnp.where(
        row == 0, jnp.sum(total_two[...].T, axis=0, keepdims=True), jnp.sum(total.T, axis=0, keepdims=True)
    )
    def block(index):
        rows = [both[24 * index + 8 * (u // 9) : 24 * index + 8 * (u // 9) + 8, tiles(u % 9)] for u in range(27)]
        last = jnp.concatenate([offsets[:, 8 * index : 8 * index + 8], jnp.zeros((8, 120), F32)], axis=1)
        return jnp.concatenate(rows + [last], axis=0)

    first = place[2] == 0
    for group in range(4):
        even, odd = (block(2 * group), block(2 * group + 1))
        turn = lax.rem(group + 4 - place[4], 4)
        keep[turn] = jnp.where(first, even, odd).astype(BF16)
        send[turn] = jnp.where(first, odd, even).astype(BF16)


def sum_of_four(parts):
    parts = [part.astype(F32) for part in parts]
    return (parts[0] + parts[2]) + (parts[1] + parts[3])


def finish_kernel(factor, first, second, third, fourth, kernel_two, kernel_one, two, one):
    total = sum_of_four([first[...], second[...], third[...], fourth[...]]) * factor
    units = [total[8 * u : 8 * u + 8] for u in range(28)]
    for dy in range(3):
        for column in range(9):
            value = units[dy * 9 + column]
            for half in range(2):
                layer, k = divmod(2 * column + half, 9)
                dz, dx = divmod(k, 3)
                target = kernel_one if layer else kernel_two
                target[dx * 9 + dy * 3 + dz] = value[:, 64 * half : 64 * half + 64]
    two[...] = units[27][0, 0:8]
    one[...] = units[27][1, 0:8]


def features_kernel(*refs):
    place = position()
    pieces, other, out, turned = (refs[:4], refs[4:8], refs[8], refs[9])
    for k in range(4):
        group = lax.rem(place[4] + 4 - k, 4)
        group = jnp.where(place[3] == 1, 3 - group, group)
        for same in range(2):
            value = (other[k][1] if same else pieces[k][0]).astype(F32)
            core = place[2] if same == 0 else 1 - place[2]
            start = pl.multiple_of(128 * (2 * group + core), 128)
            turned[pl.ds(start, 64), :] = value
            turned[pl.ds(start + 64, 64), :] = pltpu.roll(value, 64, 1)
    for o in range(8):
        out[o] = turned[pl.ds(o, 128, stride=8), :].T[0:64].astype(BF16)


def call(kernel, out_shapes, scratch, *args, scalars=(), far=(), flops=0, limit=VMEM_LIMIT):
    vmem = pl.BlockSpec(memory_space=pltpu.VMEM)
    smem = pl.BlockSpec(memory_space=pltpu.SMEM)
    anywhere = pl.BlockSpec(memory_space=pltpu.HBM)
    outs = [jax.ShapeDtypeStruct(shape, dtype) for shape, dtype in out_shapes]
    size = 0
    if flops:
        size = sum(a.size * a.dtype.itemsize for a in args)
        size += sum(o.size * o.dtype.itemsize for o in outs)
    return pl.pallas_call(
        kernel,
        out_shape=outs,
        in_specs=[smem if k in scalars else anywhere if k in far else vmem for k in range(len(args))],
        out_specs=[vmem] * len(outs),
        scratch_shapes=[pltpu.VMEM(*x) if isinstance(x, tuple) else x for x in scratch],
        compiler_params=pltpu.CompilerParams(vmem_limit_bytes=limit),
        cost_estimate=pl.CostEstimate(flops=flops, bytes_accessed=size, transcendentals=0),
    )(*args)


def neighbours():
    both = []
    for start in range(2):
        pairs = []
        for here in range(start, 31, 2):
            there = here + 1
            turn = (here // 4) % 2 != (there // 4) % 2
            for l in range(4):
                pair = (here * 4 + l, there * 4 + (3 - l if turn else l))
                pairs += [pair, pair[::-1]]
        both.append(pairs)
    return both


def shards(volume, weight_one, bias_one, weight_two, bias_two, cotangent):
    factor = float(volume.shape[1] * 32 * volume.shape[2] * volume.shape[3]) ** (-0.5)
    c = lax.axis_index("c")
    even, odd = neighbours()
    near = SPACE + ("l",)
    swap = [(0, 1), (1, 0)]

    def spread(pieces, axis="l"):
        turns = [[(i, (i + k) % 4) for i in range(4)] for k in range(4)]
        return [pieces[0]] + [lax.ppermute(pieces[k], axis, turns[k]) for k in range(1, 4)]

    def cross(pieces):
        return [lax.ppermute(piece, "c", swap) for piece in pieces]

    (pieces,) = call(
        volume_kernel,
        [((4, 2, 88, 128), BF16)],
        [((8, 64, 128), BF16), ((1072, 128), F32), pltpu.SemaphoreType.DMA(())],
        volume.reshape(8, 64, 128),
        far=(0,),
    )
    pieces = spread([pieces[k] for k in range(4)])
    rest = call(
        rest_kernel,
        [((384, 128), BF16)] * 4,
        [
            ((8, 64, 128), BF16),
            ((1072, 128), F32),
            ((2, 27, 8, 64), BF16),
            pltpu.SMEM((2, 8), F32),
            pltpu.SemaphoreType.DMA((5,)),
        ],
        cotangent.reshape(8, 64, 128),
        jnp.transpose(weight_one, (2, 3, 4, 0, 1)).reshape(27, 8, 64),
        bias_one,
        jnp.transpose(weight_two, (2, 3, 4, 0, 1)).reshape(27, 8, 64),
        bias_two,
        far=(0, 1, 2, 3, 4),
        limit=FULL_LIMIT,
    )
    rest, pieces = lax.optimization_barrier((rest, pieces))
    (field,) = call(
        unpack_kernel,
        [((11, 64, 128), BF16)],
        [],
        *pieces,
        *cross(pieces),
    )
    near_even = lax.ppermute(field, near, even)
    near_odd = lax.ppermute(field, near, odd)

    rest = spread(rest)
    weights, weights_back, bias, cots = call(
        weights_kernel,
        [((192, 1152), BF16), ((192, 576), BF16), ((2, 64, 128), F32), ((10, 64, 128), BF16)],
        [],
        *rest,
        *cross(rest),
    )

    act, wide, delta, feats, to_even, to_odd = call(
        forward_kernel,
        [
            ((192, 1536), BF16),
            ((192, 2816), BF16),
            ((10, 64, 128), BF16),
            ((4, 2, 64, 128), BF16),
            ((5, 64, 128), BF16),
            ((5, 64, 128), BF16),
        ],
        [((10, 64, 128), F32)],
        field,
        near_even,
        near_odd,
        cots,
        weights,
        bias,
        flops=2 * 192 * 576 * 128 * 30,
    )
    from_even = lax.ppermute(to_even, near, even)
    from_odd = lax.ppermute(to_odd, near, odd)
    grad_two, total_two, narrow = call(
        second_grad_kernel,
        [((192, 576), F32), ((64, 128), F32), ((192, 1280), BF16)],
        [((192, 1024), BF16)],
        delta,
        act,
        wide,
        flops=2 * 192 * 576 * 1024,
    )
    feats = spread([feats[k] for k in range(4)])
    keep, send = call(
        backward_kernel,
        [((4, 224, 128), BF16), ((4, 224, 128), BF16)],
        [((192, 1280), BF16), ((192, 1024), BF16), ((192, 1152), F32)],
        delta,
        from_even,
        from_odd,
        weights_back,
        act,
        narrow,
        grad_two,
        total_two,
        flops=4 * 192 * 576 * 1024,
    )

    other = lax.ppermute(send, "c", swap)
    parts = [(keep[k].astype(F32) + other[k].astype(F32)).astype(BF16) for k in range(4)]
    feats = feats + cross(feats)
    part = sum_of_four(spread(parts)).astype(BF16)
    other = lax.ppermute(part, "h", swap)
    other, feats = lax.optimization_barrier((other, feats))
    part = (part.astype(F32) + other.astype(F32)).astype(BF16)
    part = sum_of_four(spread([part] * 4, "y")).astype(BF16)
    parts = spread([part] * 4, "x")
    kernel_two, kernel_one, offset_two, offset_one = call(
        functools.partial(finish_kernel, factor),
        [((27, 8, 64), F32), ((27, 8, 64), F32), ((8,), F32), ((8,), F32)],
        [],
        *parts,
    )
    kernel_one, kernel_two = (
        jnp.transpose(k.reshape(3, 3, 3, 8, 64), (3, 4, 0, 1, 2)) for k in (kernel_one, kernel_two)
    )

    (features,) = call(
        features_kernel,
        [((8, 64, 128), BF16)],
        [((1024, 128), F32)],
        *feats,
    )
    return features.reshape(8, 2, 32, 128), kernel_one, offset_one, kernel_two, offset_two


def solution(mesh):
    fine = Mesh(mesh.devices.reshape(4, 2, 4, 4, 2), ("x", "h", "y", "l", "c"))
    field = P(CHAN, SPACE, None, None)
    kernel = P(CHAN, None, None, None, None)
    in_specs = (field, kernel, P(CHAN), kernel, P(CHAN), field)
    out_specs = (field, kernel, P(CHAN), kernel, P(CHAN))
    return jax.shard_map(shards, mesh=fine, in_specs=in_specs, out_specs=out_specs, check_vma=False)
```

```python
import functools

import jax
import jax.numpy as jnp
from jax import lax
from jax.experimental import pallas as pl
from jax.experimental.pallas import tpu as pltpu
from jax.sharding import Mesh, PartitionSpec as P

SLOPE = 0.2
F32 = jnp.float32
BF16 = jnp.bfloat16
SPACE = ("x", "h", "y")
PLANE = ("x", "y")
CHAN = ("l", "c")
CONTRACT_LAST = (((1,), (1,)), ((), ()))
VMEM_LIMIT = 48 * 1024 * 1024
FULL_LIMIT = 63 * 1024 * 1024


def position():
    h, l, c = (lax.axis_index(name) for name in ("h", "l", "c"))
    space = (lax.axis_index("x") * 2 + h) * 4 + lax.axis_index("y")
    block = 2 * jnp.where(h == 1, 3 - l, l) + c
    return space, block, c, h, l


def leaky(value):
    return jnp.maximum(value, SLOPE * value)


def lanes(shape):
    return lax.broadcasted_iota(jnp.int32, shape, 1)


def tiles(index, count=1):
    return slice(index * 128, (index + count) * 128)


def along_y(array, step):
    y = lanes(array.shape) % 32
    edge = 0 if step == 1 else 31
    moved = pltpu.roll(array, step % array.shape[1], 1)
    return jnp.where(y == edge, 0.0, moved)


def add_y_taps(product):
    width = product.shape[1]
    split = product.reshape(8, 3, 8, width)
    below, middle, above = (split[:, k].reshape(64, width) for k in range(3))
    return middle + along_y(below, 1) + along_y(above, -1)


def stack_y(delta):
    parts = [along_y(delta, -1), delta, along_y(delta, 1)]
    parts = [part.reshape(8, 1, 8, part.shape[1]) for part in parts]
    return jnp.concatenate(parts, axis=1).reshape(192, delta.shape[1]).astype(BF16)


def conv_tiles(weights, column, stacked, start):
    return sum(
        jnp.dot(
            weights[:, column + dz * 192 : column + dz * 192 + 192],
            stacked[:, tiles(start + dz, 2)],
            preferred_element_type=F32,
        )
        for dz in range(3)
    )


def turn_field(place, held, turned):
    turned[0:24] = jnp.zeros((24, 128), F32)
    turned[1048:1072] = jnp.zeros((24, 128), F32)
    for ch in range(8):
        value = held[ch].astype(F32)
        turned[pl.ds(24 + ch, 128, stride=8), :] = jnp.concatenate([value, value], axis=0).T


def target_of(place, block):
    chip = jnp.where(place[3] == 1, 3 - block // 2, block // 2)
    return lax.rem(chip + 4 - place[4], 4), jnp.where(place[2] == block % 2, 0, 1)


def volume_kernel(volume, out, held, turned, arrived):
    place = position()
    copy = pltpu.make_async_copy(volume, held, arrived)
    copy.start()
    low = lanes((88, 128)) < 64
    copy.wait()
    turn_field(place, held, turned)
    for block in range(8):
        turn, same = target_of(place, block)
        rows = turned[block * 128 : block * 128 + 176].reshape(11, 2, 8, 128)
        even, odd = (rows[:, k].reshape(88, 128) for k in range(2))
        out[turn, same] = jnp.where(low, even, odd).astype(BF16)


def rest_kernel(
    cotangent,
    weight_one,
    bias_one,
    weight_two,
    bias_two,
    first,
    second,
    third,
    fourth,
    held,
    turned,
    kernels,
    biases,
    arrived,
):
    place = position()
    copies = [
        pltpu.make_async_copy(ref, to, arrived.at[k])
        for k, (ref, to) in enumerate(
            (
                (cotangent, held),
                (weight_one, kernels.at[0]),
                (weight_two, kernels.at[1]),
                (bias_one, biases.at[0]),
                (bias_two, biases.at[1]),
            )
        )
    ]
    for copy in copies:
        copy.start()
    for copy in copies:
        copy.wait()

    row = lax.broadcasted_iota(jnp.int32, (8, 128), 0)
    lane = lanes((8, 128))
    rows = []
    for t in range(9):
        for dy in range(3):
            halves = []
            for half in range(2):
                layer, k = divmod(2 * t + half, 9)
                dz, dx = divmod(k, 3)
                halves.append(kernels[layer, dx * 9 + dy * 3 + dz].astype(F32))
            rows.append(jnp.concatenate(halves, axis=1))
    packed = jnp.zeros((8, 128), F32)
    for layer in range(2):
        value = sum(jnp.where(row == o, biases[layer, o], 0.0) for o in range(8))
        for part in range(3):
            rounded = value.astype(BF16).astype(F32)
            packed = jnp.where(lane == 3 * layer + part, rounded, packed)
            value = value - rounded
    rows.append(packed)
    turn_field(place, held, turned)
    low = lanes((80, 128)) < 64
    for k, out in enumerate((first, second, third, fourth)):
        chip = lax.rem(place[4] + k, 4)
        chip = jnp.where(place[3] == 1, 3 - chip, chip)
        pieces = []
        for same in range(2):
            block = 2 * chip + (1 - place[2] if same else place[2])
            start = pl.multiple_of(block * 128, 128)
            pieces.append(jnp.where(low, turned[pl.ds(start + 16, 80)], turned[pl.ds(start + 80, 80)]))
        out[...] = jnp.concatenate(pieces + rows, axis=0).astype(BF16)


def channel_order(place, ours, theirs):
    first = place[2] == 0
    pieces = [None] * 8
    pairs = [(jnp.where(first, a, b), jnp.where(first, b, a)) for a, b in zip(ours, theirs)]
    for chip in range(4):
        turn = lax.rem(place[4] + 4 - chip, 4)
        for core in range(2):
            value = pairs[3][core]
            for k in range(3):
                value = jnp.where(turn == k, pairs[k][core], value)
            pieces[2 * chip + core] = value
    return pieces


def unpack_kernel(*refs):
    place = position()
    ours, theirs, field = (refs[:4], refs[4:8], refs[8])
    ours = [ref[0].astype(F32) for ref in ours]
    theirs = [ref[1].astype(F32) for ref in theirs]
    pieces = channel_order(place, ours, theirs)
    for j in range(11):
        both = jnp.concatenate([piece[8 * j : 8 * j + 8] for piece in pieces], axis=0)
        field[j] = both.astype(BF16)


def weights_kernel(*refs):
    place = position()
    ours, theirs = (refs[:4], refs[4:8])
    out, back, bias, cots = refs[8:]
    pieces = channel_order(
        place, [ref[0:80].astype(F32) for ref in ours], [ref[80:160].astype(F32) for ref in theirs]
    )
    for j in range(10):
        both = jnp.concatenate([piece[8 * j : 8 * j + 8] for piece in pieces], axis=0)
        cots[j] = both.astype(BF16)

    first = place[2] == 0
    for k in range(4):
        group = lax.rem(place[4] + 4 - k, 4)
        mine, other = (ref[160:384].astype(F32) for ref in (ours[k], theirs[k]))
        pair = (jnp.where(first, mine, other), jnp.where(first, other, mine))
        rows = pl.ds(pl.multiple_of(48 * group, 16), 48)
        for t in range(9):
            block = jnp.concatenate([x[24 * t : 24 * t + 24] for x in pair], axis=0)
            out[rows, tiles(t)] = block.astype(BF16)
        extra = jnp.concatenate([x[216:224] for x in pair], axis=0)
        rows = pl.ds(pl.multiple_of(16 * group, 16), 16)
        for layer in range(2):
            parts = [extra[:, 3 * layer + k : 3 * layer + k + 1] for k in range(3)]
            bias[layer, rows] = jnp.broadcast_to(parts[0] + parts[1] + parts[2], (16, 128))
    kernel = out[:, 576:1152].astype(F32).reshape(8, 3, 8, 576)
    turned = [kernel[:, 2 - e].reshape(64, 576).T for e in range(3)]
    for column in range(9):
        block = [part[64 * (8 - column) : 64 * (8 - column) + 64].reshape(8, 1, 8, 64) for part in turned]
        block = jnp.concatenate(block, axis=1).reshape(192, 64)
        back[:, 64 * column : 64 * column + 64] = block.astype(BF16)


def forward_kernel(
    own, even, odd, cotangent, weights, bias, act, wide, delta, feats, to_even, to_odd, post
):
    place = position()
    upper = lax.rem(place[0], 2) == 1
    lane = lanes((64, 128))
    low = lane < 64

    for j in range(11):
        o, x, y = (ref[j].astype(F32) for ref in (own, even, odd))
        p, n = (jnp.where(upper, x, y), jnp.where(upper, y, x))
        turned = pltpu.roll(o, 64, 1)
        for half in range(2):
            if half == 0:
                minus = jnp.where(low, p, turned)
                plus = jnp.where(low, o, pltpu.roll(n, 64, 1))
            else:
                minus = jnp.where(low, pltpu.roll(p, 64, 1), o)
                plus = jnp.where(low, turned, n)
            zero = jnp.where(lane < 32, pltpu.roll(minus, 96, 1), pltpu.roll(plus, 32, 1))
            wide[0:64, tiles(2 * j + half)] = minus.astype(BF16)
            wide[64:128, tiles(2 * j + half)] = zero.astype(BF16)
            wide[128:192, tiles(2 * j + half)] = plus.astype(BF16)

    outside = jnp.logical_or(
        jnp.logical_and(lane < 32, place[0] == 0), jnp.logical_and(lane >= 96, place[0] == 31)
    )
    for m in range(10):
        product = conv_tiles(weights, 0, wide, 2 * m)
        for half in range(2):
            row = 2 * m + half
            value = leaky(add_y_taps(product[:, tiles(half)]) + bias[0])
            gone = outside
            if row < 2:
                gone = jnp.logical_or(outside, place[1] == 0)
            if row >= 18:
                gone = jnp.logical_or(outside, place[1] == 7)
            value = jnp.where(gone, 0.0, value)
            swapped = pltpu.roll(value, 64, 1).astype(BF16)
            if row < 12:
                left = slice(row * 128, row * 128 + 64)
                act[0:64, left] = value.astype(BF16)[:, 0:64]
                act[64:128, left] = pltpu.roll(value, 96, 1).astype(BF16)[:, 0:64]
                act[128:192, left] = swapped[:, 0:64]
            if row >= 8:
                right = slice((row - 8) * 128 + 64, (row - 8) * 128 + 128)
                act[0:64, right] = swapped[:, 64:128]
                act[64:128, right] = pltpu.roll(value, 32, 1).astype(BF16)[:, 64:128]
                act[128:192, right] = value.astype(BF16)[:, 64:128]

    front = lane % 64 < 32
    for m in range(5):
        product = conv_tiles(weights, 576, act, 2 * m)
        grads = []
        for half in range(2):
            row = 2 * m + half
            value = add_y_taps(product[:, tiles(half)]) + bias[1]
            cot = cotangent[row].astype(F32)
            grad = jnp.where(value > 0, cot, SLOPE * cot).astype(BF16)
            delta[row] = grad
            grads.append(grad.astype(F32))
            post[row] = leaky(value)
        to_prev = jnp.where(front, grads[0], pltpu.roll(grads[1], 32, 1))
        to_next = jnp.where(front, pltpu.roll(grads[0], 96, 1), grads[1])
        to_even[m] = jnp.where(upper, to_prev, to_next).astype(BF16)
        to_odd[m] = jnp.where(upper, to_next, to_prev).astype(BF16)

    for block in range(8):
        turn = lax.rem(block // 2 + 4 - place[4], 4)
        same = jnp.where(place[2] == block % 2, 0, 1)
        piece = [post[z + 1, 8 * block : 8 * block + 8] for z in range(8)]
        feats[turn, same] = jnp.concatenate(piece, axis=0).astype(BF16)


def kernel_grad(stacked, wide, start):
    products = [
        lax.dot_general(
            stacked[...],
            wide[:, tiles(start + dz, 8)],
            CONTRACT_LAST,
            preferred_element_type=F32,
        )
        for dz in range(3)
    ]
    return jnp.concatenate(products, axis=1)


def second_grad_kernel(delta, act, wide, out, total, narrow, stacked):
    low = lanes((192, 128)) < 64
    for k in range(8):
        value = delta[k + 1].astype(F32)
        stacked[:, tiles(k)] = stack_y(value)
        total[...] = value if k == 0 else total[...] + value
    out[...] = kernel_grad(stacked, act, 1)
    for k in range(10):
        left = pltpu.roll(wide[:, tiles(k + 2)].astype(F32), 96, 1)
        right = pltpu.roll(wide[:, tiles(k + 10)].astype(F32), 32, 1)
        narrow[:, tiles(k)] = jnp.where(low, left, right).astype(BF16)


def backward_kernel(
    delta, from_even, from_odd, weights, act, narrow, grad_two, total_two, keep, send, stacked, own, both
):
    place = position()
    lane = lanes((64, 128))
    upper = lax.rem(place[0], 2) == 1
    front = lane % 64 < 32
    for m in range(5):
        x, y = (from_even[m].astype(F32), from_odd[m].astype(F32))
        prev, after = (jnp.where(upper, x, y), jnp.where(upper, y, x))
        for half in range(2):
            row = 2 * m + half
            value = delta[row].astype(F32)
            left = pltpu.roll(prev, 96, 1) if half else prev
            right = after if half else pltpu.roll(after, 32, 1)
            minus = jnp.where(front, left, pltpu.roll(value, 32, 1))
            plus = jnp.where(front, pltpu.roll(value, 96, 1), right)
            stacked[0:64, tiles(row)] = minus.astype(BF16)
            stacked[64:128, tiles(row)] = delta[row]
            stacked[128:192, tiles(row)] = plus.astype(BF16)

    total = jnp.zeros((64, 128), F32)
    for m in range(4):
        product = conv_tiles(weights, 0, stacked, 2 * m)
        for half in range(2):
            back = add_y_taps(product[:, tiles(half)])
            positive = act[64:128, tiles(2 * m + 2 + half)].astype(F32) > 0
            value = jnp.where(positive, back, SLOPE * back).astype(BF16).astype(F32)
            own[:, tiles(2 * m + half)] = stack_y(value)
            total = total + value

    both[:, 0:576] = grad_two[...]
    both[:, 576:1152] = kernel_grad(own, narrow, 0)
    row = lax.broadcasted_iota(jnp.int32, (8, 64), 0)
    offsets = jnp.where(
        row == 0, jnp.sum(total_two[...].T, axis=0, keepdims=True), jnp.sum(total.T, axis=0, keepdims=True)
    )
    def block(index):
        rows = [both[24 * index + 8 * (u // 9) : 24 * index + 8 * (u // 9) + 8, tiles(u % 9)] for u in range(27)]
        last = jnp.concatenate([offsets[:, 8 * index : 8 * index + 8], jnp.zeros((8, 120), F32)], axis=1)
        return jnp.concatenate(rows + [last], axis=0)

    first = place[2] == 0
    for group in range(4):
        even, odd = (block(2 * group), block(2 * group + 1))
        turn = lax.rem(group + 4 - place[4], 4)
        keep[turn] = jnp.where(first, even, odd).astype(BF16)
        send[turn] = jnp.where(first, odd, even).astype(BF16)


def sum_of_four(parts):
    parts = [part.astype(F32) for part in parts]
    return (parts[0] + parts[2]) + (parts[1] + parts[3])


def finish_kernel(factor, first, second, third, fourth, kernel_two, kernel_one, two, one):
    total = sum_of_four([first[...], second[...], third[...], fourth[...]]) * factor
    units = [total[8 * u : 8 * u + 8] for u in range(28)]
    for dy in range(3):
        for column in range(9):
            value = units[dy * 9 + column]
            for half in range(2):
                layer, k = divmod(2 * column + half, 9)
                dz, dx = divmod(k, 3)
                target = kernel_one if layer else kernel_two
                target[dx * 9 + dy * 3 + dz] = value[:, 64 * half : 64 * half + 64]
    two[...] = units[27][0, 0:8]
    one[...] = units[27][1, 0:8]


def features_kernel(*refs):
    place = position()
    pieces, other, out, turned = (refs[:4], refs[4:8], refs[8], refs[9])
    for k in range(4):
        group = lax.rem(place[4] + 4 - k, 4)
        group = jnp.where(place[3] == 1, 3 - group, group)
        for same in range(2):
            value = (other[k][1] if same else pieces[k][0]).astype(F32)
            core = place[2] if same == 0 else 1 - place[2]
            start = pl.multiple_of(128 * (2 * group + core), 128)
            turned[pl.ds(start, 64), :] = value
            turned[pl.ds(start + 64, 64), :] = pltpu.roll(value, 64, 1)
    for o in range(8):
        out[o] = turned[pl.ds(o, 128, stride=8), :].T[0:64].astype(BF16)


def call(kernel, out_shapes, scratch, *args, scalars=(), far=(), flops=0, limit=VMEM_LIMIT):
    vmem = pl.BlockSpec(memory_space=pltpu.VMEM)
    smem = pl.BlockSpec(memory_space=pltpu.SMEM)
    anywhere = pl.BlockSpec(memory_space=pltpu.HBM)
    outs = [jax.ShapeDtypeStruct(shape, dtype) for shape, dtype in out_shapes]
    size = 0
    if flops:
        size = sum(a.size * a.dtype.itemsize for a in args)
        size += sum(o.size * o.dtype.itemsize for o in outs)
    return pl.pallas_call(
        kernel,
        out_shape=outs,
        in_specs=[smem if k in scalars else anywhere if k in far else vmem for k in range(len(args))],
        out_specs=[vmem] * len(outs),
        scratch_shapes=[pltpu.VMEM(*x) if isinstance(x, tuple) else x for x in scratch],
        compiler_params=pltpu.CompilerParams(vmem_limit_bytes=limit),
        cost_estimate=pl.CostEstimate(flops=flops, bytes_accessed=size, transcendentals=0),
    )(*args)


def neighbours():
    both = []
    for start in range(2):
        pairs = []
        for here in range(start, 31, 2):
            there = here + 1
            turn = (here // 4) % 2 != (there // 4) % 2
            for l in range(4):
                pair = (here * 4 + l, there * 4 + (3 - l if turn else l))
                pairs += [pair, pair[::-1]]
        both.append(pairs)
    return both


def shards(volume, weight_one, bias_one, weight_two, bias_two, cotangent):
    factor = float(volume.shape[1] * 32 * volume.shape[2] * volume.shape[3]) ** (-0.5)
    c = lax.axis_index("c")
    even, odd = neighbours()
    near = SPACE + ("l",)
    swap = [(0, 1), (1, 0)]

    def spread(pieces, axis="l"):
        turns = [[(i, (i + k) % 4) for i in range(4)] for k in range(4)]
        return [pieces[0]] + [lax.ppermute(pieces[k], axis, turns[k]) for k in range(1, 4)]

    def cross(pieces):
        return [lax.ppermute(piece, "c", swap) for piece in pieces]

    (pieces,) = call(
        volume_kernel,
        [((4, 2, 88, 128), BF16)],
        [((8, 64, 128), BF16), ((1072, 128), F32), pltpu.SemaphoreType.DMA(())],
        volume.reshape(8, 64, 128),
        far=(0,),
    )
    pieces = spread([pieces[k] for k in range(4)])
    rest = call(
        rest_kernel,
        [((384, 128), BF16)] * 4,
        [
            ((8, 64, 128), BF16),
            ((1072, 128), F32),
            ((2, 27, 8, 64), BF16),
            pltpu.SMEM((2, 8), F32),
            pltpu.SemaphoreType.DMA((5,)),
        ],
        cotangent.reshape(8, 64, 128),
        jnp.transpose(weight_one, (2, 3, 4, 0, 1)).reshape(27, 8, 64),
        bias_one,
        jnp.transpose(weight_two, (2, 3, 4, 0, 1)).reshape(27, 8, 64),
        bias_two,
        far=(0, 1, 2, 3, 4),
        limit=FULL_LIMIT,
    )
    rest, pieces = lax.optimization_barrier((rest, pieces))
    (field,) = call(
        unpack_kernel,
        [((11, 64, 128), BF16)],
        [],
        *pieces,
        *cross(pieces),
    )
    near_even = lax.ppermute(field, near, even)
    near_odd = lax.ppermute(field, near, odd)

    rest = spread(rest)
    weights, weights_back, bias, cots = call(
        weights_kernel,
        [((192, 1152), BF16), ((192, 576), BF16), ((2, 64, 128), F32), ((10, 64, 128), BF16)],
        [],
        *rest,
        *cross(rest),
    )

    act, wide, delta, feats, to_even, to_odd = call(
        forward_kernel,
        [
            ((192, 1536), BF16),
            ((192, 2816), BF16),
            ((10, 64, 128), BF16),
            ((4, 2, 64, 128), BF16),
            ((5, 64, 128), BF16),
            ((5, 64, 128), BF16),
        ],
        [((10, 64, 128), F32)],
        field,
        near_even,
        near_odd,
        cots,
        weights,
        bias,
        flops=2 * 192 * 576 * 128 * 30,
    )
    from_odd = lax.ppermute(to_odd, near, odd)
    from_even = lax.ppermute(to_even, near, even)
    grad_two, total_two, narrow = call(
        second_grad_kernel,
        [((192, 576), F32), ((64, 128), F32), ((192, 1280), BF16)],
        [((192, 1024), BF16)],
        delta,
        act,
        wide,
        flops=2 * 192 * 576 * 1024,
    )
    feats = spread([feats[k] for k in range(4)])
    keep, send = call(
        backward_kernel,
        [((4, 224, 128), BF16), ((4, 224, 128), BF16)],
        [((192, 1280), BF16), ((192, 1024), BF16), ((192, 1152), F32)],
        delta,
        from_even,
        from_odd,
        weights_back,
        act,
        narrow,
        grad_two,
        total_two,
        flops=4 * 192 * 576 * 1024,
    )

    other = lax.ppermute(send, "c", swap)
    parts = [(keep[k].astype(F32) + other[k].astype(F32)).astype(BF16) for k in range(4)]
    feats = feats + cross(feats)
    part = sum_of_four(spread(parts)).astype(BF16)
    other = lax.ppermute(part, "h", swap)
    other, feats = lax.optimization_barrier((other, feats))
    part = (part.astype(F32) + other.astype(F32)).astype(BF16)
    part = sum_of_four(spread([part] * 4, "y")).astype(BF16)
    parts = spread([part] * 4, "x")
    kernel_two, kernel_one, offset_two, offset_one = call(
        functools.partial(finish_kernel, factor),
        [((27, 8, 64), F32), ((27, 8, 64), F32), ((8,), F32), ((8,), F32)],
        [],
        *parts,
    )
    kernel_one, kernel_two = (
        jnp.transpose(k.reshape(3, 3, 3, 8, 64), (3, 4, 0, 1, 2)) for k in (kernel_one, kernel_two)
    )

    (features,) = call(
        features_kernel,
        [((8, 64, 128), BF16)],
        [((1024, 128), F32)],
        *feats,
    )
    return features.reshape(8, 2, 32, 128), kernel_one, offset_one, kernel_two, offset_two


def solution(mesh):
    fine = Mesh(mesh.devices.reshape(4, 2, 4, 4, 2), ("x", "h", "y", "l", "c"))
    field = P(CHAN, SPACE, None, None)
    kernel = P(CHAN, None, None, None, None)
    in_specs = (field, kernel, P(CHAN), kernel, P(CHAN), field)
    out_specs = (field, kernel, P(CHAN), kernel, P(CHAN))
    return jax.shard_map(shards, mesh=fine, in_specs=in_specs, out_specs=out_specs, check_vma=False)
```
